32 devices in a mesh: user: 8 (over y, x, core), item: 4 (over z).
Axes of the slice: x: 2, y: 2, z: 4, core: 2. Of those that a mesh axis runs over, the one named last changes fastest.
Arguments:
- ratings: bfloat16 [6144, 6144], P('user', 'item')
- presence: int32 [48, 48], P('user', 'item'), may hold values from 0 to 1
- user_factors: float32 [6144, 128], P('user'), may hold values from -4 to 4
- item_factors: float32 [6144, 128], P('item'), may hold values from -4 to 4
- step_sizes: float32 [2], replicated, may hold values from 0.3 to 0.7
Outputs:
- new_users: float32 [6144, 128], P('user')
- new_items: float32 [6144, 128], P('item')
The draws below stay inside these ranges and needn't reach their ends.
All inputs are finite; a program needn't handle non-finite values.
Results may differ from the reference program's by a relative error of at most 0.0003.
Values sent between devices are 32-bit elements; how exact they have to be, the bound alone decides.
A program may use at most 64 MiB of HBM per device.

```python
import jax
import jax.numpy as jnp
from jax import lax

K = 128
BLK = 128
USERS = 6144
ITEMS = 6144
UBLK = 48
IBLK = 48


def draw_presence(key, part):
    first, second, third = jax.random.split(jax.random.fold_in(key, 11), 3)
    row_level = jax.random.randint(first, (UBLK, 1), 1, 9)
    col_level = jax.random.randint(second, (1, IBLK), 0, 8)
    rolled = jax.random.randint(third, (UBLK, IBLK), 0, 16)
    return (rolled < row_level + col_level).astype(jnp.int32)


def draw_ratings(key, part):
    first = jax.random.fold_in(jax.random.fold_in(key, 23), 0)
    spread = 0.5 * jnp.sqrt(jnp.float32(ITEMS) / 2.0)
    values = jnp.clip(jax.random.normal(first, (USERS, ITEMS), jnp.float32), -6.0, 6.0) * spread
    return values.astype(jnp.bfloat16)


def levels(rng, dims, pieces, smallest, largest):
    level = 1.0
    for dim, parts in pieces:
        heights = jax.random.uniform(jax.random.fold_in(jax.random.fold_in(rng, 6), dim), (parts,), jnp.float32, smallest / len(pieces), largest / len(pieces))
        level = level * jnp.repeat(jnp.exp(heights), dims[dim] // parts).reshape((-1,) + (1,) * (len(dims) - 1 - dim))
    return level


def noise(own_key, extent, width, reach, cuts=(), dtype=jnp.bfloat16):
    values = jax.random.normal(own_key, extent, jnp.float32) * width
    if len(cuts) > 0:
        values = levels(own_key, extent, cuts, -0.22, 0.18) * values
    return jnp.clip(values, min=-reach, max=reach).astype(dtype)


def setup_inputs(seed: int = 0) -> dict:
    arg_keys = jax.random.split(jax.random.key(seed), 6)
    return {
        "ratings": draw_ratings(jax.random.fold_in(arg_keys[5], 71), 0),
        "presence": draw_presence(jax.random.fold_in(arg_keys[5], 71), 0),
        "user_factors": noise(arg_keys[2], (USERS, K), 1.0, 4.0, ((0, 8),), jnp.float32),
        "item_factors": noise(arg_keys[3], (ITEMS, K), 1.0, 4.0, ((0, 4),), jnp.float32),
        "step_sizes": jnp.clip(jax.random.uniform(arg_keys[4], (2,), jnp.float32, 0.3, 0.7), 0.3, 0.7),
    }


highest = lax.Precision.HIGHEST

def block_residual(rating_rows, mask_row, user_rows, item_factors):
    predicted = jnp.dot(user_rows, item_factors.T, precision=highest, preferred_element_type=jnp.float32)
    present = jnp.repeat(mask_row.astype(jnp.float32), BLK)
    return (rating_rows.astype(jnp.float32) - predicted) * present[None, :]

def reference(ratings, presence, user_factors, item_factors, step_sizes):
    user_blocks = USERS // BLK
    rating_blocks = ratings.reshape(user_blocks, BLK, ITEMS)
    users = user_factors.reshape(user_blocks, BLK, K)
    user_scale = step_sizes[0] / (BLK * (1.0 + lax.optimization_barrier(jnp.sum(presence, axis=1)).astype(jnp.float32)))
    item_scale = step_sizes[1] / (BLK * (1.0 + lax.optimization_barrier(jnp.sum(presence, axis=0)).astype(jnp.float32)))
    item_scale = jnp.repeat(item_scale, BLK)

    def user_grad(packed):
        rating_rows, mask_row, user_rows = packed
        resid = block_residual(rating_rows, mask_row, user_rows, item_factors)
        return jnp.dot(resid, item_factors, precision=highest, preferred_element_type=jnp.float32)
    for sweep in range(2):
        gradients = lax.map(user_grad, (rating_blocks, presence, users))
        users = users + gradients * user_scale[:, None, None]

    def add_block(running, packed):
        rating_rows, mask_row, user_rows = packed
        resid = block_residual(rating_rows, mask_row, user_rows, item_factors)
        return (running + jnp.dot(resid.T, user_rows, precision=highest, preferred_element_type=jnp.float32), None)
    summed, _ = lax.scan(add_block, jnp.zeros((ITEMS, K), jnp.float32), (rating_blocks, presence, users))
    new_items = item_factors + summed * item_scale[:, None]
    return (users.reshape(USERS, K), new_items)
```

```python
import functools

import jax
import jax.numpy as jnp
from jax import lax
from jax.experimental import pallas as pl
from jax.experimental.pallas import tpu as pltpu
from jax.sharding import PartitionSpec as P

BLK = 128
f32 = jnp.float32
bf16 = jnp.bfloat16
MESH = pl.DeviceIdType.MESH


def split(x):
    hi = x.astype(bf16)
    lo = (x - hi.astype(f32)).astype(bf16)
    return hi, lo


def both(x):
    return jnp.concatenate(split(x), axis=1)


def fold(x):
    k = x.shape[1] // 2
    return x[:, :k] + x[:, k:]


def dot3(x, y):
    xh, xl = split(x)
    yh, yl = split(y)
    return jnp.dot(
        jnp.concatenate([xh, xl, xh], axis=1),
        jnp.concatenate([yh, yh, yl], axis=0),
        preferred_element_type=f32,
    )


def gram(pair):
    full = lax.dot_general(pair, pair, (((0,), (0,)), ((), ())), preferred_element_type=f32)
    k = full.shape[0] // 2
    full = full[:k] + full[k:]
    return full[:, :k] + full[:, k:]


def kernel(
    nu,
    ni,
    r_ref,
    p_ref,
    u_ref,
    q_ref,
    step_ref,
    ou_ref,
    oi_ref,
    qq,
    qg,
    masked,
    masked_t,
    mask_row,
    part,
    rs_in,
    pp,
    hs,
    acc,
    scale,
    cc_out,
    cc_in,
    *rest,
):
    levels = nu.bit_length() - 1
    halves = rest[:levels]
    (rs_s, rs_r, ag_s, ag_r, cc_s, cc_r, hv_s, hv_r, db_s, db_r) = rest[levels:]
    ub, _, k = u_ref.shape
    items = q_ref.shape[0]
    ib = items // BLK
    h = ub // 2
    u = lax.axis_index("user")
    z = lax.axis_index("item")

    barrier = pltpu.get_barrier_semaphore()
    for d in range(1, nu):
        pl.semaphore_signal(barrier, inc=1, device_id=(lax.rem(u + d, nu), z), device_id_type=MESH)

    @pl.when(z > 0)
    def _():
        pl.semaphore_signal(barrier, inc=1, device_id=(u, z - 1), device_id_type=MESH)

    @pl.when(z < ni - 1)
    def _():
        pl.semaphore_signal(barrier, inc=1, device_id=(u, z + 1), device_id_type=MESH)

    def rs_copy(b, to):
        return pltpu.make_async_remote_copy(
            src_ref=part.at[b],
            dst_ref=rs_in.at[b],
            send_sem=rs_s.at[b],
            recv_sem=rs_r.at[b],
            device_id=(u, to),
            device_id_type=MESH,
        )

    def ag_copy(b, to):
        return pltpu.make_async_remote_copy(
            src_ref=ou_ref.at[b],
            dst_ref=ou_ref.at[b],
            send_sem=ag_s.at[b],
            recv_sem=ag_r.at[b],
            device_id=(u, to),
            device_id_type=MESH,
        )

    def cc_copy(d):
        return pltpu.make_async_remote_copy(
            src_ref=cc_out,
            dst_ref=cc_in.at[d - 1],
            send_sem=cc_s.at[d - 1],
            recv_sem=cc_r.at[d - 1],
            device_id=(lax.rem(u + d, nu), z),
            device_id_type=MESH,
        )

    left = jnp.maximum(z - 1, 0)
    right = jnp.minimum(z + 1, ni - 1)

    @pl.loop(0, ib)
    def _(i):
        rows = pl.ds(pl.multiple_of(i * BLK, BLK), BLK)
        pair = both(q_ref[rows, :])
        qq[rows, :] = pair
        qg[i] = gram(pair)
        hs[i] = jnp.zeros((k, k), f32)
        count = p_ref[0, i]
        for b in range(1, ub):
            count = count + p_ref[b, i]
        cc_out[pl.ds(i, 1), :] = jnp.full((1, k), count.astype(f32), f32)

    pl.semaphore_wait(barrier, nu - 1 + jnp.minimum(z, 1) + jnp.minimum(ni - 1 - z, 1))

    @pl.loop(0, ub)
    def _(m):
        b = m // 2 + (m % 2) * h
        rows = pl.ds(pl.multiple_of(b * BLK, BLK), BLK)
        total = p_ref[b, 0]
        grams = jnp.zeros((k, k), f32)
        for i in range(ib):
            present = p_ref[b, i].astype(f32)
            mask_row[:, i * BLK : (i + 1) * BLK] = jnp.full((8, BLK), present, f32)
            grams = grams + present * qg[i]
            if i:
                total = total + p_ref[b, i]
        kept = r_ref[rows, :] * mask_row[0:1, :].astype(bf16)
        masked[b] = kept
        part[b, 0:BLK] = fold(jnp.dot(kept, qq[...], preferred_element_type=f32))
        part[b, BLK : BLK + k] = grams
        part[b, BLK + k : BLK + k + 8] = jnp.full((8, k), total.astype(f32), f32)

        @pl.when(jnp.logical_and(z == ni - 1, b < h))
        def _():
            rs_copy(b, left).start()

        @pl.when(jnp.logical_and(z == 0, b >= h))
        def _():
            rs_copy(b, right).start()

    for d in range(1, nu):
        cc_copy(d).start()

    def finish(b):
        a = part[b, 0:BLK]
        g = part[b, BLK : BLK + k]
        s = step_ref[0] / (BLK * (1.0 + part[b, BLK + k : BLK + k + 1]))
        p = u_ref[b]
        p = p + s * (a - dot3(p, g))
        p = p + s * (a - dot3(p, g))
        ou_ref[b] = p

    def use(b):
        pair = both(ou_ref[b])
        pp[pl.ds(pl.multiple_of(b * BLK, BLK), BLK), :] = pair
        g = gram(pair)
        for i in range(ib):
            hs[i] = hs[i] + p_ref[b, i].astype(f32) * g

    def reduce_step(j, b, frm, to, away, last):
        @pl.when(jnp.logical_and(away, jnp.logical_and(j >= 0, j < h)))
        def _():
            rs_copy(b, frm).wait_recv()
            part[b] = part[b] + rs_in[b]

            @pl.when(jnp.logical_not(last))
            def _():
                rs_copy(b, to).start()

            @pl.when(last)
            def _():
                finish(b)
                ag_copy(b, frm).start()
                use(b)

    def gather_step(j, b, frm, to, away, last):
        @pl.when(jnp.logical_and(away, jnp.logical_and(j >= 0, j < h)))
        def _():
            ag_copy(b, frm).wait_recv()

            @pl.when(jnp.logical_not(last))
            def _():
                ag_copy(b, to).start()

            use(b)

    def transpose_block(b):
        masked_t[:, pl.ds(pl.multiple_of(b * BLK, BLK), BLK)] = masked[b].T

    steps = 2 * (ni - 1) + h
    first, end = z == 0, z == ni - 1
    inner_first, inner_end = z > 0, z < ni - 1

    @pl.loop(1, steps)
    def _(t):
        j = t - z
        reduce_step(j, jnp.clip(j, 0, h - 1) + h, left, right, inner_first, end)
        j = t - (ni - 1 - z)
        reduce_step(j, jnp.clip(j, 0, h - 1), right, left, inner_end, first)
        j = t - (ni - 1) - z
        gather_step(j, jnp.clip(j, 0, h - 1), left, right, inner_first, end)
        j = t - 2 * (ni - 1) + z
        gather_step(j, jnp.clip(j, 0, h - 1) + h, right, left, inner_end, first)

        @pl.when(t - 1 < ub)
        def _():
            transpose_block(jnp.minimum(t - 1, ub - 1))

    for b in range(steps - 1, ub):
        transpose_block(b)

    bits = [(u // (1 << i)) % 2 for i in range(levels)]
    partners = [u + (1 << i) * (1 - 2 * bits[i]) for i in range(levels)]
    core = bits[0]

    def pick(xs, level):
        if level == 0:
            return xs[0]
        one, two = xs[level], xs[levels - level]
        return one + core * (two - one)

    size = items
    start = 0
    plan = []
    for level in range(levels):
        size = size // 2
        bit = pick(bits, level)
        keep = pl.multiple_of(start + bit * size, 8)
        send = pl.multiple_of(start + (1 - bit) * size, 8)
        plan.append((size, keep, send, pick(partners, level)))
        start = keep

    def half_copy(level):
        n, _, send, to = plan[level]
        return pltpu.make_async_remote_copy(
            src_ref=acc.at[pl.ds(send, n)],
            dst_ref=halves[level],
            send_sem=hv_s.at[level],
            recv_sem=hv_r.at[level],
            device_id=(to, z),
            device_id_type=MESH,
        )

    def double_copy(level):
        n, keep, _, to = plan[level]
        return pltpu.make_async_remote_copy(
            src_ref=oi_ref.at[pl.ds(keep, n)],
            dst_ref=oi_ref.at[pl.ds(keep, n)],
            send_sem=db_s.at[level],
            recv_sem=db_r.at[level],
            device_id=(to, z),
            device_id_type=MESH,
        )

    def product(base, n):
        rows = pl.ds(pl.multiple_of(base, BLK), n)
        acc[rows, :] = fold(jnp.dot(masked_t[rows, :], pp[...], preferred_element_type=f32))
        for m in range(n // BLK):
            block = base // BLK + m
            own = pl.ds(pl.multiple_of(base + m * BLK, BLK), BLK)
            acc[own, :] = acc[own, :] - dot3(q_ref[own, :], hs[block])

    n, keep, send, _ = plan[0]
    product(send, n)
    half_copy(0).start()
    product(keep, n)

    for d in range(1, nu):
        cc_copy(d).wait_recv()
    counts = cc_out[...]
    for d in range(1, nu):
        counts = counts + cc_in[d - 1]
    scaling = step_ref[1] / (BLK * (1.0 + counts))
    for i in range(ib):
        scale[i * BLK : (i + 1) * BLK, :] = jnp.broadcast_to(scaling[i : i + 1], (BLK, k))

    for level in range(levels):
        n, keep, _, _ = plan[level]
        if level:
            half_copy(level).start()
        half_copy(level).wait_recv()
        rows = pl.ds(keep, n)
        if level < levels - 1:
            acc[rows, :] = acc[rows, :] + halves[level][...]
        else:
            oi_ref[rows, :] = q_ref[rows, :] + (acc[rows, :] + halves[level][...]) * scale[rows, :]

    for level in reversed(range(levels)):
        double_copy(level).start()
        n, keep, send, to = plan[level]
        double_copy(level).wait_recv()

    for level in range(levels):
        half_copy(level).wait_send()
        double_copy(level).wait_send()
    for d in range(1, nu):
        cc_copy(d).wait_send()

    @pl.loop(0, h)
    def _(b):
        @pl.when(z > 0)
        def _():
            rs_copy(b, left).wait_send()
            ag_copy(b + h, left).wait_send()

        @pl.when(z < ni - 1)
        def _():
            rs_copy(b + h, right).wait_send()
            ag_copy(b, right).wait_send()


def solution(mesh):
    nu, ni = mesh.shape["user"], mesh.shape["item"]

    def body(ratings, presence, user_factors, item_factors, step_sizes):
        users, items = ratings.shape
        k = item_factors.shape[1]
        ub, ib = users // BLK, items // BLK
        levels = nu.bit_length() - 1
        ibp = -(-ib // 8) * 8
        vm = pl.BlockSpec(memory_space=pltpu.VMEM)
        sm = pl.BlockSpec(memory_space=pltpu.SMEM)
        dma = pltpu.SemaphoreType.DMA
        new_users, new_items = pl.pallas_call(
            functools.partial(kernel, nu, ni),
            out_shape=(
                jax.ShapeDtypeStruct((ub, BLK, k), f32),
                jax.ShapeDtypeStruct((items, k), f32),
            ),
            in_specs=[vm, sm, vm, vm, sm],
            out_specs=(vm, vm),
            scratch_shapes=[
                pltpu.VMEM((items, 2 * k), bf16),
                pltpu.VMEM((ib, k, k), f32),
                pltpu.VMEM((ub, BLK, items), bf16),
                pltpu.VMEM((items, users), bf16),
                pltpu.VMEM((8, items), f32),
                pltpu.VMEM((ub, BLK + k + 8, k), f32),
                pltpu.VMEM((ub, BLK + k + 8, k), f32),
                pltpu.VMEM((users, 2 * k), bf16),
                pltpu.VMEM((ib, k, k), f32),
                pltpu.VMEM((items, k), f32),
                pltpu.VMEM((items, k), f32),
                pltpu.VMEM((ibp, k), f32),
                pltpu.VMEM((nu - 1, ibp, k), f32),
            ]
            + [pltpu.VMEM((items >> (i + 1), k), f32) for i in range(levels)]
            + [
                dma((ub,)),
                dma((ub,)),
                dma((ub,)),
                dma((ub,)),
                dma((nu - 1,)),
                dma((nu - 1,)),
                dma((levels,)),
                dma((levels,)),
                dma((levels,)),
                dma((levels,)),
            ],
            compiler_params=pltpu.CompilerParams(
                collective_id=0, has_side_effects=True, vmem_limit_bytes=40 * 2**20
            ),
            cost_estimate=pl.CostEstimate(
                flops=8 * users * items * k, bytes_accessed=2 * users * items, transcendentals=0
            ),
        )(ratings, presence, user_factors.reshape(ub, BLK, k), item_factors, step_sizes)
        return new_users.reshape(users, k), new_items

    return jax.shard_map(
        body,
        mesh=mesh,
        in_specs=(P("user", "item"), P("user", "item"), P("user", None), P("item", None), P()),
        out_specs=(P("user", None), P("item", None)),
        check_vma=False,
    )
```

```python
import functools

import jax
import jax.numpy as jnp
from jax import lax
from jax.experimental import pallas as pl
from jax.experimental.pallas import tpu as pltpu
from jax.sharding import PartitionSpec as P

BLK = 128
f32 = jnp.float32
bf16 = jnp.bfloat16
MESH = pl.DeviceIdType.MESH


def split(x):
    hi = x.astype(bf16)
    lo = (x - hi.astype(f32)).astype(bf16)
    return hi, lo


def both(x):
    return jnp.concatenate(split(x), axis=1)


def fold(x):
    k = x.shape[1] // 2
    return x[:, :k] + x[:, k:]


def dot3(x, y):
    xh, xl = split(x)
    yh, yl = split(y)
    return jnp.dot(
        jnp.concatenate([xh, xl, xh], axis=1),
        jnp.concatenate([yh, yh, yl], axis=0),
        preferred_element_type=f32,
    )


def gram(pair):
    full = lax.dot_general(pair, pair, (((0,), (0,)), ((), ())), preferred_element_type=f32)
    k = full.shape[0] // 2
    full = full[:k] + full[k:]
    return full[:, :k] + full[:, k:]


def grid_of(rows, k):
    row = lax.broadcasted_iota(jnp.int32, (rows, k), 0)
    lane = lax.broadcasted_iota(jnp.int32, (rows, k), 1)
    return row, lane


def pack(g):
    k = g.shape[0]
    n = k // 2
    row, lane = grid_of(n, k)
    low = g[n:]
    packed = jnp.where(lane < row, pltpu.roll(low, n, 1), g[:n])
    diagonal = jnp.sum(jnp.where(lane == row + n, low, 0.0), axis=0, keepdims=True)
    return packed, diagonal


def unpack(packed, diagonal):
    n, k = packed.shape
    row, lane = grid_of(n, k)
    upper = jnp.where(lane > row, packed, 0.0)
    lower = pltpu.roll(jnp.where(lane < row, packed, 0.0), n, 1)
    once = jnp.concatenate([upper, lower], axis=0)
    top = jnp.where(lane == row, packed, 0.0)
    bottom = jnp.where(lane == row + n, diagonal, 0.0)
    return once + once.T + jnp.concatenate([top, bottom], axis=0)


def kernel(
    nu,
    ni,
    r_hbm,
    p_hbm,
    u_hbm,
    q_hbm,
    step_hbm,
    ou_ref,
    oi_ref,
    r_ref,
    p_ref,
    u_ref,
    q_ref,
    step_ref,
    qq,
    qg,
    masked,
    masked_t,
    mask_row,
    part,
    rs_in,
    pp,
    hs,
    acc,
    scale,
    cc_out,
    cc_in,
    *rest,
):
    levels = nu.bit_length() - 1
    halves = rest[:levels]
    (in_s, row_s, rs_s, rs_r, ag_s, ag_r, cc_s, cc_r, hv_s, hv_r, db_s, db_r) = rest[levels:]
    ub, _, k = u_ref.shape
    items = q_ref.shape[0]
    ib = items // BLK
    h = ub // 2
    half = BLK // 2
    kh = k // 2
    sub = part.shape[1]
    cut = sub - kh - 8
    u = lax.axis_index("user")
    z = lax.axis_index("item")

    inputs = [
        pltpu.make_async_copy(src, dst, in_s.at[n])
        for n, (src, dst) in enumerate(
            ((q_hbm, q_ref), (p_hbm, p_ref), (step_hbm, step_ref), (u_hbm, u_ref))
        )
    ]
    for copy in inputs:
        copy.start()

    def fetch(b):
        rows = pl.ds(pl.multiple_of(b * BLK, BLK), BLK)
        return pltpu.make_async_copy(r_hbm.at[rows], r_ref.at[b], row_s.at[b])

    late = z // ((ni + 1) // 2)

    def ordered(m):
        return lax.rem(m + (1 - late) * h, ub)

    for m in range(ub):
        fetch(ordered(m)).start()

    barrier = pltpu.get_barrier_semaphore()
    for d in range(1, nu):
        pl.semaphore_signal(barrier, inc=1, device_id=(lax.rem(u + d, nu), z), device_id_type=MESH)

    @pl.when(z > 0)
    def _():
        pl.semaphore_signal(barrier, inc=1, device_id=(u, z - 1), device_id_type=MESH)

    @pl.when(z < ni - 1)
    def _():
        pl.semaphore_signal(barrier, inc=1, device_id=(u, z + 1), device_id_type=MESH)

    def rs_copy(b, to):
        return pltpu.make_async_remote_copy(
            src_ref=part.at[b],
            dst_ref=rs_in.at[b],
            send_sem=rs_s.at[b],
            recv_sem=rs_r.at[b],
            device_id=(u, to),
            device_id_type=MESH,
        )

    def ag_copy(b, to):
        return pltpu.make_async_remote_copy(
            src_ref=ou_ref.at[b],
            dst_ref=ou_ref.at[b],
            send_sem=ag_s.at[b],
            recv_sem=ag_r.at[b],
            device_id=(u, to),
            device_id_type=MESH,
        )

    def cc_copy(d):
        return pltpu.make_async_remote_copy(
            src_ref=cc_out,
            dst_ref=cc_in.at[d - 1],
            send_sem=cc_s.at[d - 1],
            recv_sem=cc_r.at[d - 1],
            device_id=(lax.rem(u + d, nu), z),
            device_id_type=MESH,
        )

    left = jnp.maximum(z - 1, 0)
    right = jnp.minimum(z + 1, ni - 1)

    for copy in inputs:
        copy.wait()

    @pl.loop(0, ib)
    def _(i):
        rows = pl.ds(pl.multiple_of(i * BLK, BLK), BLK)
        pair = both(q_ref[rows, :])
        qq[rows, :] = pair
        qg[i] = gram(pair)
        hs[i] = jnp.zeros((k, k), f32)
        count = p_ref[0, i]
        for b in range(1, ub):
            count = count + p_ref[b, i]
        cc_out[pl.ds(i, 1), :] = jnp.full((1, k), count.astype(f32), f32)

    pl.semaphore_wait(barrier, nu - 1 + jnp.minimum(z, 1) + jnp.minimum(ni - 1 - z, 1))

    @pl.loop(0, ub)
    def _(m):
        b = ordered(m)
        total = p_ref[b, 0]
        grams = jnp.zeros((k, k), f32)
        for i in range(ib):
            present = p_ref[b, i].astype(f32)
            mask_row[:, i * BLK : (i + 1) * BLK] = jnp.full((8, BLK), present, f32)
            grams = grams + present * qg[i]
            if i:
                total = total + p_ref[b, i]
        fetch(b).wait()
        kept = r_ref[b] * mask_row[0:1, :].astype(bf16)
        masked[b] = kept
        a = fold(jnp.dot(kept, qq[...], preferred_element_type=f32))
        packed, diagonal = pack(grams)
        part[2 * b, 0:kh] = packed
        part[2 * b, kh : kh + 1] = diagonal
        part[2 * b, kh + 1 : kh + 8] = jnp.full((7, k), total.astype(f32), f32)
        part[2 * b, kh + 8 : sub] = a[:cut]
        part[2 * b + 1, 0 : BLK - cut] = a[cut:]

        @pl.when(jnp.logical_and(z == ni - 1, b < h))
        def _():
            rs_copy(2 * b, left).start()
            rs_copy(2 * b + 1, left).start()

        @pl.when(jnp.logical_and(z == 0, b >= h))
        def _():
            rs_copy(2 * b, right).start()
            rs_copy(2 * b + 1, right).start()

    for d in range(1, nu):
        cc_copy(d).start()

    def finish(b):
        a = jnp.concatenate([part[2 * b, kh + 8 : sub], part[2 * b + 1, 0 : BLK - cut]], axis=0)
        g = unpack(part[2 * b, 0:kh], part[2 * b, kh : kh + 1])
        gh, gl = split(g)
        gs = jnp.concatenate([gh, gh, gl], axis=0)
        s = step_ref[0] / (BLK * (1.0 + part[2 * b, kh + 1 : kh + 2]))
        p = u_ref[b]
        for _ in range(2):
            ph, pl_ = split(p)
            ps = jnp.concatenate([ph, pl_, ph], axis=1)
            p = p + s * (a - jnp.dot(ps, gs, preferred_element_type=f32))
        ou_ref[2 * b] = p[:half]
        ou_ref[2 * b + 1] = p[half:]

    def use(b):
        pair = both(jnp.concatenate([ou_ref[2 * b], ou_ref[2 * b + 1]], axis=0))
        pp[pl.ds(pl.multiple_of(b * BLK, BLK), BLK), :] = pair
        g = gram(pair)
        for i in range(ib):
            hs[i] = hs[i] + p_ref[b, i].astype(f32) * g

    def valid(j, away):
        return jnp.logical_and(away, jnp.logical_and(j >= 0, j < 2 * h))

    def reduce_step(j, c, frm, to, away, last):
        @pl.when(valid(j, away))
        def _():
            rs_copy(c, frm).wait_recv()
            part[c] = part[c] + rs_in[c]

            @pl.when(jnp.logical_not(last))
            def _():
                rs_copy(c, to).start()

    def finish_step(j, c, frm, away, last):
        done = jnp.logical_and(last, j % 2 == 1)

        @pl.when(jnp.logical_and(valid(j, away), done))
        def _():
            finish(c // 2)
            ag_copy(c - 1, frm).start()
            ag_copy(c, frm).start()
            use(c // 2)

    def gather_step(j, c, frm, to, away, last):
        @pl.when(valid(j, away))
        def _():
            ag_copy(c, frm).wait_recv()

            @pl.when(jnp.logical_not(last))
            def _():
                ag_copy(c, to).start()

    def use_step(j, c, away):
        @pl.when(jnp.logical_and(valid(j, away), j % 2 == 1))
        def _():
            use(c // 2)

    def transpose_block(b):
        masked_t[:, pl.ds(pl.multiple_of(b * BLK, BLK), BLK)] = masked[b].T

    steps = 2 * ni + 2 * h - 1
    first, end = z == 0, z == ni - 1
    inner_first, inner_end = z > 0, z < ni - 1

    def low(j):
        return jnp.clip(j, 0, 2 * h - 1)

    def high(j):
        return low(j) + 2 * h

    @pl.loop(1, steps)
    def _(t):
        jr = t - z
        jl = t - (ni - 1 - z)
        gl = t - ni - z
        gr = t - ni - (ni - 1 - z)
        reduce_step(jr, high(jr), left, right, inner_first, end)
        reduce_step(jl, low(jl), right, left, inner_end, first)
        gather_step(gl, low(gl), left, right, inner_first, end)
        gather_step(gr, high(gr), right, left, inner_end, first)
        finish_step(jr, high(jr), left, inner_first, end)
        finish_step(jl, low(jl), right, inner_end, first)
        use_step(gl, low(gl), inner_first)
        use_step(gr, high(gr), inner_end)

        @pl.when(t - 1 < ub)
        def _():
            transpose_block(jnp.minimum(t - 1, ub - 1))

    for b in range(steps - 1, ub):
        transpose_block(b)

    bits = [(u // (1 << i)) % 2 for i in range(levels)]
    partners = [u + (1 << i) * (1 - 2 * bits[i]) for i in range(levels)]
    core = bits[0]

    def pick(xs, level):
        if level == 0:
            return xs[0]
        one, two = xs[level], xs[levels - level]
        return one + core * (two - one)

    size = items
    start = 0
    plan = []
    for level in range(levels):
        size = size // 2
        bit = pick(bits, level)
        keep = pl.multiple_of(start + bit * size, 8)
        send = pl.multiple_of(start + (1 - bit) * size, 8)
        plan.append((size, keep, send, pick(partners, level)))
        start = keep

    def half_copy(level):
        n, _, send, to = plan[level]
        return pltpu.make_async_remote_copy(
            src_ref=acc.at[pl.ds(send, n)],
            dst_ref=halves[level],
            send_sem=hv_s.at[level],
            recv_sem=hv_r.at[level],
            device_id=(to, z),
            device_id_type=MESH,
        )

    def double_copy(level):
        n, keep, _, to = plan[level]
        return pltpu.make_async_remote_copy(
            src_ref=oi_ref.at[pl.ds(keep, n)],
            dst_ref=oi_ref.at[pl.ds(keep, n)],
            send_sem=db_s.at[level],
            recv_sem=db_r.at[level],
            device_id=(to, z),
            device_id_type=MESH,
        )

    def product(base, n):
        rows = pl.ds(pl.multiple_of(base, BLK), n)
        acc[rows, :] = fold(jnp.dot(masked_t[rows, :], pp[...], preferred_element_type=f32))
        for m in range(n // BLK):
            block = base // BLK + m
            own = pl.ds(pl.multiple_of(base + m * BLK, BLK), BLK)
            acc[own, :] = acc[own, :] - dot3(q_ref[own, :], hs[block])

    n, keep, send, _ = plan[0]
    product(send, n)
    half_copy(0).start()
    product(keep, n)

    for d in range(1, nu):
        cc_copy(d).wait_recv()
    counts = cc_out[...]
    for d in range(1, nu):
        counts = counts + cc_in[d - 1]
    scaling = step_ref[1] / (BLK * (1.0 + counts))
    for i in range(ib):
        scale[i * BLK : (i + 1) * BLK, :] = jnp.broadcast_to(scaling[i : i + 1], (BLK, k))

    for level in range(levels):
        n, keep, _, _ = plan[level]
        if level:
            half_copy(level).start()
        half_copy(level).wait_recv()
        rows = pl.ds(keep, n)
        if level < levels - 1:
            acc[rows, :] = acc[rows, :] + halves[level][...]
        else:
            oi_ref[rows, :] = q_ref[rows, :] + (acc[rows, :] + halves[level][...]) * scale[rows, :]

    for level in reversed(range(levels)):
        double_copy(level).start()
        n, keep, send, to = plan[level]
        double_copy(level).wait_recv()

    for level in range(levels):
        half_copy(level).wait_send()
        double_copy(level).wait_send()
    for d in range(1, nu):
        cc_copy(d).wait_send()

    @pl.loop(0, 2 * h)
    def _(c):
        @pl.when(z > 0)
        def _():
            rs_copy(c, left).wait_send()
            ag_copy(c + 2 * h, left).wait_send()

        @pl.when(z < ni - 1)
        def _():
            rs_copy(c + 2 * h, right).wait_send()
            ag_copy(c, right).wait_send()


def solution(mesh):
    nu, ni = mesh.shape["user"], mesh.shape["item"]

    def body(ratings, presence, user_factors, item_factors, step_sizes):
        users, items = ratings.shape
        k = item_factors.shape[1]
        ub, ib = users // BLK, items // BLK
        levels = nu.bit_length() - 1
        ibp = -(-ib // 8) * 8
        sub = -(-(BLK + k // 2 + 8) // 16) * 8
        vm = pl.BlockSpec(memory_space=pltpu.VMEM)
        hbm = pl.BlockSpec(memory_space=pltpu.HBM)
        dma = pltpu.SemaphoreType.DMA
        new_users, new_items = pl.pallas_call(
            functools.partial(kernel, nu, ni),
            out_shape=(
                jax.ShapeDtypeStruct((2 * ub, BLK // 2, k), f32),
                jax.ShapeDtypeStruct((items, k), f32),
            ),
            in_specs=[hbm] * 5,
            out_specs=(vm, vm),
            scratch_shapes=[
                pltpu.VMEM((ub, BLK, items), bf16),
                pltpu.SMEM((ub, ib), jnp.int32),
                pltpu.VMEM((ub, BLK, k), f32),
                pltpu.VMEM((items, k), f32),
                pltpu.SMEM((2,), f32),
                pltpu.VMEM((items, 2 * k), bf16),
                pltpu.VMEM((ib, k, k), f32),
                pltpu.VMEM((ub, BLK, items), bf16),
                pltpu.VMEM((items, users), bf16),
                pltpu.VMEM((8, items), f32),
                pltpu.VMEM((2 * ub, sub, k), f32),
                pltpu.VMEM((2 * ub, sub, k), f32),
                pltpu.VMEM((users, 2 * k), bf16),
                pltpu.VMEM((ib, k, k), f32),
                pltpu.VMEM((items, k), f32),
                pltpu.VMEM((items, k), f32),
                pltpu.VMEM((ibp, k), f32),
                pltpu.VMEM((nu - 1, ibp, k), f32),
            ]
            + [pltpu.VMEM((items >> (i + 1), k), f32) for i in range(levels)]
            + [
                dma((4,)),
                dma((ub,)),
                dma((2 * ub,)),
                dma((2 * ub,)),
                dma((2 * ub,)),
                dma((2 * ub,)),
                dma((nu - 1,)),
                dma((nu - 1,)),
                dma((levels,)),
                dma((levels,)),
                dma((levels,)),
                dma((levels,)),
            ],
            compiler_params=pltpu.CompilerParams(
                collective_id=0, has_side_effects=True, vmem_limit_bytes=56 * 2**20
            ),
            cost_estimate=pl.CostEstimate(
                flops=8 * users * items * k, bytes_accessed=2 * users * items, transcendentals=0
            ),
        )(ratings, presence, user_factors.reshape(ub, BLK, k), item_factors, step_sizes)
        return new_users.reshape(users, k), new_items

    return jax.shard_map(
        body,
        mesh=mesh,
        in_specs=(P("user", "item"), P("user", "item"), P("user", None), P("item", None), P()),
        out_specs=(P("user", None), P("item", None)),
        check_vma=False,
    )
```

```python
import functools

import jax
import jax.numpy as jnp
from jax import lax
from jax.experimental import pallas as pl
from jax.experimental.pallas import tpu as pltpu
from jax.sharding import PartitionSpec as P

BLK = 128
f32 = jnp.float32
bf16 = jnp.bfloat16
MESH = pl.DeviceIdType.MESH


def split(x):
    hi = x.astype(bf16)
    lo = (x - hi.astype(f32)).astype(bf16)
    return hi, lo


def both(x):
    return jnp.concatenate(split(x), axis=1)


def fold(x):
    k = x.shape[1] // 2
    return x[:, :k] + x[:, k:]


def three(x):
    hi, lo = split(x)
    return jnp.concatenate([hi, hi, lo], axis=0)


def stacked(x):
    return jnp.concatenate(split(x.T), axis=0)


def gram(stack, pair):
    full = jnp.dot(stack, pair, preferred_element_type=f32)
    k = full.shape[0] // 2
    full = full[:k] + full[k:]
    return full[:, :k] + full[:, k:]


def grid_of(rows, k):
    row = lax.broadcasted_iota(jnp.int32, (rows, k), 0)
    lane = lax.broadcasted_iota(jnp.int32, (rows, k), 1)
    return row, lane


def pack(g):
    k = g.shape[0]
    n = k // 2
    row, lane = grid_of(n, k)
    low = g[n:]
    packed = jnp.where(lane < row, pltpu.roll(low, n, 1), g[:n])
    diagonal = jnp.sum(jnp.where(lane == row + n, low, 0.0), axis=0, keepdims=True)
    return packed, diagonal


def unpack(packed, diagonal):
    n, k = packed.shape
    row, lane = grid_of(n, k)
    upper = jnp.where(lane > row, packed, 0.0)
    lower = pltpu.roll(jnp.where(lane < row, packed, 0.0), n, 1)
    once = jnp.concatenate([upper, lower], axis=0)
    top = jnp.where(lane == row, packed, 0.0)
    bottom = jnp.where(lane == row + n, diagonal, 0.0)
    return once + once.T + jnp.concatenate([top, bottom], axis=0)


def kernel(
    nu,
    ni,
    r_hbm,
    p_hbm,
    u_hbm,
    q_hbm,
    step_hbm,
    ou_ref,
    oi_ref,
    r_ref,
    p_ref,
    u_ref,
    q_ref,
    step_ref,
    qq,
    qg,
    masked,
    mask_row,
    part,
    rs_in,
    ppt,
    hs,
    acc,
    scale,
    cc_out,
    cc_in,
    *rest,
):
    levels = nu.bit_length() - 1
    halves = rest[:levels]
    (in_s, row_s, rs_s, rs_r, ag_s, ag_r, cc_s, cc_r, hv_s, hv_r, db_s, db_r) = rest[levels:]
    ub, _, k = u_ref.shape
    items = q_ref.shape[0]
    ib = items // BLK
    h = ub // 2
    half = BLK // 2
    kh = k // 2
    sub = part.shape[1]
    cut = sub - kh - 8
    u = lax.axis_index("user")
    z = lax.axis_index("item")

    inputs = [
        pltpu.make_async_copy(src, dst, in_s.at[n])
        for n, (src, dst) in enumerate(
            ((q_hbm, q_ref), (p_hbm, p_ref), (step_hbm, step_ref), (u_hbm, u_ref))
        )
    ]
    for copy in inputs:
        copy.start()

    def fetch(b):
        rows = pl.ds(pl.multiple_of(b * BLK, BLK), BLK)
        return pltpu.make_async_copy(r_hbm.at[rows], r_ref.at[b], row_s.at[b])

    late = z // ((ni + 1) // 2)

    def ordered(m):
        return lax.rem(m + (1 - late) * h, ub)

    for m in range(ub):
        fetch(ordered(m)).start()

    barrier = pltpu.get_barrier_semaphore()
    for d in range(1, nu):
        pl.semaphore_signal(barrier, inc=1, device_id=(lax.rem(u + d, nu), z), device_id_type=MESH)

    @pl.when(z > 0)
    def _():
        pl.semaphore_signal(barrier, inc=1, device_id=(u, z - 1), device_id_type=MESH)

    @pl.when(z < ni - 1)
    def _():
        pl.semaphore_signal(barrier, inc=1, device_id=(u, z + 1), device_id_type=MESH)

    def rs_copy(b, to):
        return pltpu.make_async_remote_copy(
            src_ref=part.at[b],
            dst_ref=rs_in.at[b],
            send_sem=rs_s.at[b],
            recv_sem=rs_r.at[b],
            device_id=(u, to),
            device_id_type=MESH,
        )

    def ag_copy(b, to):
        return pltpu.make_async_remote_copy(
            src_ref=ou_ref.at[b],
            dst_ref=ou_ref.at[b],
            send_sem=ag_s.at[b],
            recv_sem=ag_r.at[b],
            device_id=(u, to),
            device_id_type=MESH,
        )

    def cc_copy(d):
        return pltpu.make_async_remote_copy(
            src_ref=cc_out,
            dst_ref=cc_in.at[d - 1],
            send_sem=cc_s.at[d - 1],
            recv_sem=cc_r.at[d - 1],
            device_id=(lax.rem(u + d, nu), z),
            device_id_type=MESH,
        )

    left = jnp.maximum(z - 1, 0)
    right = jnp.minimum(z + 1, ni - 1)

    for copy in inputs:
        copy.wait()

    for i in range(ib):
        rows = pl.ds(i * BLK, BLK)
        own = q_ref[rows, :]
        pair = both(own)
        qq[rows, :] = pair
        qg[i] = gram(stacked(own), pair)
    hs[...] = jnp.zeros_like(hs)
    for i in range(ib):
        count = p_ref[0, i]
        for b in range(1, ub):
            count = count + p_ref[b, i]
        cc_out[pl.ds(i, 1), :] = jnp.full((1, k), count.astype(f32), f32)

    pl.semaphore_wait(barrier, nu - 1 + jnp.minimum(z, 1) + jnp.minimum(ni - 1 - z, 1))

    @pl.loop(0, 2)
    def _(m):
        base = lax.rem(m + 1 - late, 2) * h
        for n in range(h):
            b = base + n
            total = p_ref[b, 0]
            grams = jnp.zeros((k, k), f32)
            for i in range(ib):
                present = p_ref[b, i].astype(f32)
                mask_row[n : n + 1, i * BLK : (i + 1) * BLK] = jnp.full((1, BLK), present, f32)
                grams = grams + present * qg[i]
                if i:
                    total = total + p_ref[b, i]
            packed, diagonal = pack(grams)
            part[2 * b, 0:kh] = packed
            part[2 * b, kh : kh + 1] = diagonal
            part[2 * b, kh + 1 : kh + 8] = jnp.full((7, k), total.astype(f32), f32)
        for n in range(h):
            fetch(base + n).wait()
        for n in range(h):
            b = base + n
            rows = pl.ds(pl.multiple_of(b * BLK, BLK), BLK)
            masked[rows, :] = r_ref[b] * mask_row[n : n + 1, :].astype(bf16)
        rows = pl.ds(pl.multiple_of(base * BLK, BLK), h * BLK)
        a = fold(jnp.dot(masked[rows, :], qq[...], preferred_element_type=f32))
        for n in range(h):
            b = base + n
            part[2 * b, kh + 8 : sub] = a[n * BLK : n * BLK + cut]
            part[2 * b + 1, 0 : BLK - cut] = a[n * BLK + cut : (n + 1) * BLK]

        @pl.when(jnp.logical_and(z == ni - 1, base == 0))
        def _():
            for n in range(2 * h):
                rs_copy(2 * base + n, left).start()

        @pl.when(jnp.logical_and(z == 0, base == h))
        def _():
            for n in range(2 * h):
                rs_copy(2 * base + n, right).start()

    for d in range(1, nu):
        cc_copy(d).start()

    def finish(b):
        a = jnp.concatenate([part[2 * b, kh + 8 : sub], part[2 * b + 1, 0 : BLK - cut]], axis=0)
        g = unpack(part[2 * b, 0:kh], part[2 * b, kh : kh + 1])
        gs = three(g)
        s = step_ref[0] / (BLK * (1.0 + part[2 * b, kh + 1 : kh + 2]))
        p = u_ref[b]
        for _ in range(2):
            ph, pl_ = split(p)
            ps = jnp.concatenate([ph, pl_, ph], axis=1)
            p = p + s * (a - jnp.dot(ps, gs, preferred_element_type=f32))
        ou_ref[2 * b] = p[:half]
        ou_ref[2 * b + 1] = p[half:]

    def use(b):
        own = jnp.concatenate([ou_ref[2 * b], ou_ref[2 * b + 1]], axis=0)
        stack = stacked(own)
        ppt[:, pl.ds(pl.multiple_of(b * BLK, BLK), BLK)] = stack
        g = gram(stack, both(own))
        for i in range(ib):
            hs[i] = hs[i] + p_ref[b, i].astype(f32) * g

    def valid(j, away):
        return jnp.logical_and(away, jnp.logical_and(j >= 0, j < 2 * h))

    def reduce_step(j, c, frm, to, away, last):
        @pl.when(valid(j, away))
        def _():
            rs_copy(c, frm).wait_recv()
            part[c] = part[c] + rs_in[c]

            @pl.when(jnp.logical_not(last))
            def _():
                rs_copy(c, to).start()

    def finish_step(j, c, frm, away, last):
        done = jnp.logical_and(last, j % 2 == 1)

        @pl.when(jnp.logical_and(valid(j, away), done))
        def _():
            finish(c // 2)
            ag_copy(c - 1, frm).start()
            ag_copy(c, frm).start()
            use(c // 2)

    def gather_step(j, c, frm, to, away, last):
        @pl.when(valid(j, away))
        def _():
            ag_copy(c, frm).wait_recv()

            @pl.when(jnp.logical_not(last))
            def _():
                ag_copy(c, to).start()

    def use_step(j, c, away):
        @pl.when(jnp.logical_and(valid(j, away), j % 2 == 1))
        def _():
            use(c // 2)

    steps = 2 * ni + 2 * h - 1
    first, end = z == 0, z == ni - 1
    inner_first, inner_end = z > 0, z < ni - 1

    def low(j):
        return jnp.clip(j, 0, 2 * h - 1)

    def high(j):
        return low(j) + 2 * h

    @pl.loop(1, steps)
    def _(t):
        jr = t - z
        jl = t - (ni - 1 - z)
        gl = t - ni - z
        gr = t - ni - (ni - 1 - z)
        reduce_step(jr, high(jr), left, right, inner_first, end)
        reduce_step(jl, low(jl), right, left, inner_end, first)
        finish_step(jr, high(jr), left, inner_first, end)
        finish_step(jl, low(jl), right, inner_end, first)
        gather_step(gl, low(gl), left, right, inner_first, end)
        gather_step(gr, high(gr), right, left, inner_end, first)
        use_step(gl, low(gl), inner_first)
        use_step(gr, high(gr), inner_end)

    bits = [(u // (1 << i)) % 2 for i in range(levels)]
    partners = [u + (1 << i) * (1 - 2 * bits[i]) for i in range(levels)]
    core = bits[0]

    def pick(xs, level):
        if level == 0:
            return xs[0]
        one, two = xs[level], xs[levels - level]
        return one + core * (two - one)

    size = items
    start = 0
    plan = []
    for level in range(levels):
        size = size // 2
        bit = pick(bits, level)
        keep = pl.multiple_of(start + bit * size, 8)
        send = pl.multiple_of(start + (1 - bit) * size, 8)
        plan.append((size, keep, send, pick(partners, level)))
        start = keep

    def half_copy(level):
        n, _, send, to = plan[level]
        return pltpu.make_async_remote_copy(
            src_ref=acc.at[pl.ds(send, n)],
            dst_ref=halves[level],
            send_sem=hv_s.at[level],
            recv_sem=hv_r.at[level],
            device_id=(to, z),
            device_id_type=MESH,
        )

    def double_copy(level):
        n, keep, _, to = plan[level]
        return pltpu.make_async_remote_copy(
            src_ref=oi_ref.at[pl.ds(keep, n)],
            dst_ref=oi_ref.at[pl.ds(keep, n)],
            send_sem=db_s.at[level],
            recv_sem=db_r.at[level],
            device_id=(to, z),
            device_id_type=MESH,
        )

    def product(base, n):
        base = pl.multiple_of(base, BLK)
        wide = jnp.dot(ppt[...], masked[:, pl.ds(base, n)], preferred_element_type=f32)
        wide = wide[:k] + wide[k:]
        for m in range(n // BLK):
            rows = pl.ds(pl.multiple_of(base + m * BLK, BLK), BLK)
            pair = qq[rows, :]
            left_side = jnp.concatenate([pair, pair[:, :k]], axis=1)
            known = jnp.dot(left_side, three(hs[base // BLK + m]), preferred_element_type=f32)
            acc[rows, :] = wide[:, m * BLK : (m + 1) * BLK].T - known

    n, keep, send, _ = plan[0]
    product(send, n)
    half_copy(0).start()
    product(keep, n)

    for d in range(1, nu):
        cc_copy(d).wait_recv()
    counts = cc_out[...]
    for d in range(1, nu):
        counts = counts + cc_in[d - 1]
    scaling = step_ref[1] / (BLK * (1.0 + counts))
    for i in range(ib):
        scale[i * BLK : (i + 1) * BLK, :] = jnp.broadcast_to(scaling[i : i + 1], (BLK, k))

    for level in range(levels):
        n, keep, _, _ = plan[level]
        if level:
            half_copy(level).start()
        half_copy(level).wait_recv()
        rows = pl.ds(keep, n)
        if level < levels - 1:
            acc[rows, :] = acc[rows, :] + halves[level][...]
        else:
            oi_ref[rows, :] = q_ref[rows, :] + (acc[rows, :] + halves[level][...]) * scale[rows, :]

    for level in reversed(range(levels)):
        double_copy(level).start()
        n, keep, send, to = plan[level]
        double_copy(level).wait_recv()

    for level in range(levels):
        half_copy(level).wait_send()
        double_copy(level).wait_send()
    for d in range(1, nu):
        cc_copy(d).wait_send()

    @pl.loop(0, 2 * h)
    def _(c):
        @pl.when(z > 0)
        def _():
            rs_copy(c, left).wait_send()
            ag_copy(c + 2 * h, left).wait_send()

        @pl.when(z < ni - 1)
        def _():
            rs_copy(c + 2 * h, right).wait_send()
            ag_copy(c, right).wait_send()


def solution(mesh):
    nu, ni = mesh.shape["user"], mesh.shape["item"]

    def body(ratings, presence, user_factors, item_factors, step_sizes):
        users, items = ratings.shape
        k = item_factors.shape[1]
        ub, ib = users // BLK, items // BLK
        levels = nu.bit_length() - 1
        ibp = -(-ib // 8) * 8
        sub = -(-(BLK + k // 2 + 8) // 16) * 8
        vm = pl.BlockSpec(memory_space=pltpu.VMEM)
        hbm = pl.BlockSpec(memory_space=pltpu.HBM)
        dma = pltpu.SemaphoreType.DMA
        new_users, new_items = pl.pallas_call(
            functools.partial(kernel, nu, ni),
            out_shape=(
                pltpu.VMEM((2 * ub, BLK // 2, k), f32),
                pltpu.VMEM((items, k), f32),
            ),
            in_specs=[hbm] * 5,
            out_specs=(vm, vm),
            scratch_shapes=[
                pltpu.VMEM((ub, BLK, items), bf16),
                pltpu.SMEM((ub, ib), jnp.int32),
                pltpu.VMEM((ub, BLK, k), f32),
                pltpu.VMEM((items, k), f32),
                pltpu.SMEM((2,), f32),
                pltpu.VMEM((items, 2 * k), bf16),
                pltpu.VMEM((ib, k, k), f32),
                pltpu.VMEM((users, items), bf16),
                pltpu.VMEM((-(-ub // 16) * 8, items), f32),
                pltpu.VMEM((2 * ub, sub, k), f32),
                pltpu.VMEM((2 * ub, sub, k), f32),
                pltpu.VMEM((2 * k, users), bf16),
                pltpu.VMEM((ib, k, k), f32),
                pltpu.VMEM((items, k), f32),
                pltpu.VMEM((items, k), f32),
                pltpu.VMEM((ibp, k), f32),
                pltpu.VMEM((nu - 1, ibp, k), f32),
            ]
            + [pltpu.VMEM((items >> (i + 1), k), f32) for i in range(levels)]
            + [
                dma((4,)),
                dma((ub,)),
                dma((2 * ub,)),
                dma((2 * ub,)),
                dma((2 * ub,)),
                dma((2 * ub,)),
                dma((nu - 1,)),
                dma((nu - 1,)),
                dma((levels,)),
                dma((levels,)),
                dma((levels,)),
                dma((levels,)),
            ],
            compiler_params=pltpu.CompilerParams(
                collective_id=0, has_side_effects=True, vmem_limit_bytes=56 * 2**20
            ),
            cost_estimate=pl.CostEstimate(
                flops=8 * users * items * k, bytes_accessed=2 * users * items, transcendentals=0
            ),
        )(ratings, presence, user_factors.reshape(ub, BLK, k), item_factors, step_sizes)
        return new_users.reshape(users, k), new_items

    return jax.shard_map(
        body,
        mesh=mesh,
        in_specs=(P("user", "item"), P("user", "item"), P("user", None), P("item", None), P()),
        out_specs=(P("user", None), P("item", None)),
        check_vma=False,
    )
```

```python
import functools
import itertools

import jax
import jax.numpy as jnp
from jax import lax
from jax.experimental import pallas as pl
from jax.experimental.pallas import tpu as pltpu
from jax.sharding import PartitionSpec as P

BLK = 128
LAG = 3
f32 = jnp.float32
bf16 = jnp.bfloat16
MESH = pl.DeviceIdType.MESH


def split(x):
    hi = x.astype(bf16)
    lo = (x - hi.astype(f32)).astype(bf16)
    return hi, lo


def both(x):
    return jnp.concatenate(split(x), axis=1)


def fold(x):
    k = x.shape[1] // 2
    return x[:, :k] + x[:, k:]


def three(x):
    hi, lo = split(x)
    return jnp.concatenate([hi, hi, lo], axis=0)


def stacked(x):
    return jnp.concatenate(split(x.T), axis=0)


def gram(stack, pair):
    full = jnp.dot(stack, pair, preferred_element_type=f32)
    k = full.shape[0] // 2
    full = full[:k] + full[k:]
    return full[:, :k] + full[:, k:]


def grid_of(rows, k):
    row = lax.broadcasted_iota(jnp.int32, (rows, k), 0)
    lane = lax.broadcasted_iota(jnp.int32, (rows, k), 1)
    return row, lane


def pack(g):
    k = g.shape[0]
    n = k // 2
    row, lane = grid_of(n, k)
    low = g[n:]
    packed = jnp.where(lane < row, pltpu.roll(low, n, 1), g[:n])
    diagonal = jnp.sum(jnp.where(lane == row + n, low, 0.0), axis=0, keepdims=True)
    return packed, diagonal


def unpack(packed, diagonal):
    n, k = packed.shape
    row, lane = grid_of(n, k)
    upper = jnp.where(lane > row, packed, 0.0)
    lower = pltpu.roll(jnp.where(lane < row, packed, 0.0), n, 1)
    once = jnp.concatenate([upper, lower], axis=0)
    top = jnp.where(lane == row, packed, 0.0)
    bottom = jnp.where(lane == row + n, diagonal, 0.0)
    return once + once.T + jnp.concatenate([top, bottom], axis=0)


def kernel(
    nu,
    ni,
    r_hbm,
    p_hbm,
    u_hbm,
    q_hbm,
    step_hbm,
    ou_ref,
    oi_ref,
    r_ref,
    p_ref,
    u_ref,
    q_ref,
    step_ref,
    qq,
    qg,
    masked,
    mask_row,
    part,
    rs_in,
    ppt,
    hs,
    acc,
    scale,
    cc_out,
    cc_in,
    halves,
    *rest,
):
    levels = nu.bit_length() - 1
    (in_s, row_s, rs_s, rs_r, ag_s, ag_r, cc_s, cc_r, hv_s, hv_r, db_s, db_r) = rest
    ub, _, k = u_ref.shape
    items = q_ref.shape[0]
    ib = items // BLK
    h = ub // 2
    half = BLK // 2
    kh = k // 2
    sub = part.shape[1]
    cut = sub - kh - 8
    u = lax.axis_index("user")
    z = lax.axis_index("item")

    inputs = [
        pltpu.make_async_copy(src, dst, in_s.at[n])
        for n, (src, dst) in enumerate(
            ((q_hbm, q_ref), (p_hbm, p_ref), (step_hbm, step_ref), (u_hbm, u_ref))
        )
    ]
    for copy in inputs:
        copy.start()

    def fetch(b):
        rows = pl.ds(pl.multiple_of(b * BLK, BLK), BLK)
        return pltpu.make_async_copy(r_hbm.at[rows], r_ref.at[b], row_s.at[b])

    late = z // ((ni + 1) // 2)

    def ordered(m):
        return lax.rem(m + (1 - late) * h, ub)

    for m in range(ub):
        fetch(ordered(m)).start()

    barrier = pltpu.get_barrier_semaphore()
    for d in range(1, nu):
        pl.semaphore_signal(barrier, inc=1, device_id=(lax.rem(u + d, nu), z), device_id_type=MESH)

    @pl.when(z > 0)
    def _():
        pl.semaphore_signal(barrier, inc=1, device_id=(u, z - 1), device_id_type=MESH)

    @pl.when(z < ni - 1)
    def _():
        pl.semaphore_signal(barrier, inc=1, device_id=(u, z + 1), device_id_type=MESH)

    def rs_copy(b, to):
        return pltpu.make_async_remote_copy(
            src_ref=part.at[b],
            dst_ref=rs_in.at[b],
            send_sem=rs_s.at[b],
            recv_sem=rs_r.at[b],
            device_id=(u, to),
            device_id_type=MESH,
        )

    def ag_copy(b, to):
        return pltpu.make_async_remote_copy(
            src_ref=ou_ref.at[b],
            dst_ref=ou_ref.at[b],
            send_sem=ag_s.at[b],
            recv_sem=ag_r.at[b],
            device_id=(u, to),
            device_id_type=MESH,
        )

    def cc_copy(d):
        return pltpu.make_async_remote_copy(
            src_ref=cc_out,
            dst_ref=cc_in.at[d - 1],
            send_sem=cc_s.at[d - 1],
            recv_sem=cc_r.at[d - 1],
            device_id=(lax.rem(u + d, nu), z),
            device_id_type=MESH,
        )

    left = jnp.maximum(z - 1, 0)
    right = jnp.minimum(z + 1, ni - 1)

    for copy in inputs:
        copy.wait()

    for i in range(ib):
        rows = pl.ds(i * BLK, BLK)
        own = q_ref[rows, :]
        pair = both(own)
        qq[rows, :] = pair
        qg[i] = gram(stacked(own), pair)
    hs[...] = jnp.zeros_like(hs)
    for i in range(ib):
        count = p_ref[0, i]
        for b in range(1, ub):
            count = count + p_ref[b, i]
        cc_out[pl.ds(i, 1), :] = jnp.full((1, k), count.astype(f32), f32)

    pl.semaphore_wait(barrier, nu - 1 + jnp.minimum(z, 1) + jnp.minimum(ni - 1 - z, 1))

    @pl.loop(0, 2)
    def _(m):
        base = lax.rem(m + 1 - late, 2) * h
        for n in range(h):
            b = base + n
            total = p_ref[b, 0]
            grams = jnp.zeros((k, k), f32)
            for i in range(ib):
                present = p_ref[b, i].astype(f32)
                mask_row[n : n + 1, i * BLK : (i + 1) * BLK] = jnp.full((1, BLK), present, f32)
                grams = grams + present * qg[i]
                if i:
                    total = total + p_ref[b, i]
            packed, diagonal = pack(grams)
            part[2 * b, 0:kh] = packed
            part[2 * b, kh : kh + 1] = diagonal
            part[2 * b, kh + 1 : kh + 8] = jnp.full((7, k), total.astype(f32), f32)
        for n in range(h):
            fetch(base + n).wait()
        for n in range(h):
            b = base + n
            rows = pl.ds(pl.multiple_of(b * BLK, BLK), BLK)
            masked[rows, :] = r_ref[b] * mask_row[n : n + 1, :].astype(bf16)
        rows = pl.ds(pl.multiple_of(base * BLK, BLK), h * BLK)
        a = fold(jnp.dot(masked[rows, :], qq[...], preferred_element_type=f32))
        for n in range(h):
            b = base + n
            part[2 * b, kh + 8 : sub] = a[n * BLK : n * BLK + cut]
            part[2 * b + 1, 0 : BLK - cut] = a[n * BLK + cut : (n + 1) * BLK]

        @pl.when(jnp.logical_and(z == ni - 1, base == 0))
        def _():
            for n in range(2 * h):
                rs_copy(2 * base + n, left).start()

        @pl.when(jnp.logical_and(z == 0, base == h))
        def _():
            for n in range(2 * h):
                rs_copy(2 * base + n, right).start()

    for d in range(1, nu):
        cc_copy(d).start()

    def finish(b):
        a = jnp.concatenate([part[2 * b, kh + 8 : sub], part[2 * b + 1, 0 : BLK - cut]], axis=0)
        g = unpack(part[2 * b, 0:kh], part[2 * b, kh : kh + 1])
        gs = three(g)
        s = step_ref[0] / (BLK * (1.0 + part[2 * b, kh + 1 : kh + 2]))
        p = u_ref[b]
        for _ in range(2):
            ph, pl_ = split(p)
            ps = jnp.concatenate([ph, pl_, ph], axis=1)
            p = p + s * (a - jnp.dot(ps, gs, preferred_element_type=f32))
        ou_ref[2 * b] = p[:half]
        ou_ref[2 * b + 1] = p[half:]

    def use(b):
        own = jnp.concatenate([ou_ref[2 * b], ou_ref[2 * b + 1]], axis=0)
        stack = stacked(own)
        ppt[:, pl.ds(pl.multiple_of(b * BLK, BLK), BLK)] = stack
        g = gram(stack, both(own))
        for i in range(ib):
            hs[i] = hs[i] + p_ref[b, i].astype(f32) * g

    def valid(j, away):
        return jnp.logical_and(away, jnp.logical_and(j >= 0, j < 2 * h))

    def reduce_step(j, c, frm, to, away, last):
        @pl.when(valid(j, away))
        def _():
            rs_copy(c, frm).wait_recv()
            part[c] = part[c] + rs_in[c]

            @pl.when(jnp.logical_not(last))
            def _():
                rs_copy(c, to).start()

    def finish_step(j, c, frm, away, last):
        done = jnp.logical_and(last, j % 2 == 1)

        @pl.when(jnp.logical_and(valid(j, away), done))
        def _():
            finish(c // 2)
            ag_copy(c - 1, frm).start()
            ag_copy(c, frm).start()
            use(c // 2)

    def gather_step(j, c, frm, to, away, last):
        @pl.when(valid(j, away))
        def _():
            ag_copy(c, frm).wait_recv()

            @pl.when(jnp.logical_not(last))
            def _():
                ag_copy(c, to).start()

    def use_step(j, c, away):
        @pl.when(jnp.logical_and(valid(j, away), j % 2 == 1))
        def _():
            use(c // 2)

    far = LAG * (ni - 1)
    first, end = z == 0, z == ni - 1
    inner_first, inner_end = z > 0, z < ni - 1

    def low(j):
        return jnp.clip(j, 0, 2 * h - 1)

    def high(j):
        return low(j) + 2 * h

    @pl.loop(LAG, 2 * far + 2 * h + 1)
    def _(t):
        jr = t - LAG * z
        jl = t - (far - LAG * z)
        gl = t - far - 1 - LAG * z
        gr = t - far - 1 - (far - LAG * z)
        reduce_step(jr, high(jr), left, right, inner_first, end)
        reduce_step(jl, low(jl), right, left, inner_end, first)
        finish_step(jr, high(jr), left, inner_first, end)
        finish_step(jl, low(jl), right, inner_end, first)
        gather_step(gl, low(gl), left, right, inner_first, end)
        gather_step(gr, high(gr), right, left, inner_end, first)
        use_step(gl, low(gl), inner_first)
        use_step(gr, high(gr), inner_end)

    bits = [(u // (1 << i)) % 2 for i in range(levels)]
    partners = [u + (1 << i) * (1 - 2 * bits[i]) for i in range(levels)]
    core = bits[0]

    def pick(xs, level, which):
        if level == 0:
            return xs[0]
        one, two = xs[level], xs[levels - level]
        return one + which * (two - one)

    mine = [pick(bits, n, core) for n in range(levels)]
    theirs = [pick(bits, n, 1 - core) for n in range(levels)]
    to = [pick(partners, n, core) for n in range(levels)]
    leaf = items >> levels
    offset = [sum(1 << (levels - m - 1) for m in range(n)) for n in range(levels)]

    def tails(level):
        return list(itertools.product((0, 1), repeat=levels - level - 1))

    def place(level, tail):
        number = 0
        for f in tail:
            number = 2 * number + f
        return offset[level] + number

    def rows_of(digits):
        start = 0
        for n, d in enumerate(digits):
            start = start + d * (items >> (n + 1))
        return pl.ds(pl.multiple_of(start, 8), leaf)

    def turned(known, tail):
        ahead = known[levels - len(tail) :] if tail else []
        return [1 - d if f else d for d, f in zip(ahead, tail)]

    def sent(level, tail):
        known = mine if level else theirs
        return rows_of(mine[:level] + [1 - mine[level]] + turned(known, tail))

    def held(level, tail):
        return rows_of(mine[: level + 1] + turned(mine, tail))

    def half_copy(level, tail):
        n = place(level, tail)
        return pltpu.make_async_remote_copy(
            src_ref=acc.at[sent(level, tail)],
            dst_ref=halves.at[n],
            send_sem=hv_s.at[n],
            recv_sem=hv_r.at[n],
            device_id=(to[level], z),
            device_id_type=MESH,
        )

    def double_copy(level, tail):
        n = place(level, tail)
        rows = held(level, tail)
        return pltpu.make_async_remote_copy(
            src_ref=oi_ref.at[rows],
            dst_ref=oi_ref.at[rows],
            send_sem=db_s.at[n],
            recv_sem=db_r.at[n],
            device_id=(to[level], z),
            device_id_type=MESH,
        )

    def product(base, n):
        base = pl.multiple_of(base, BLK)
        wide = jnp.dot(ppt[...], masked[:, pl.ds(base, n)], preferred_element_type=f32)
        wide = wide[:k] + wide[k:]
        for m in range(n // BLK):
            rows = pl.ds(pl.multiple_of(base + m * BLK, BLK), BLK)
            pair = qq[rows, :]
            left_side = jnp.concatenate([pair, pair[:, :k]], axis=1)
            known = jnp.dot(left_side, three(hs[base // BLK + m]), preferred_element_type=f32)
            acc[rows, :] = wide[:, m * BLK : (m + 1) * BLK].T - known

    quarter = items // 4
    for f in (1, 0):
        second = 1 - theirs[1] if f else theirs[1]
        product((1 - mine[0]) * 2 * quarter + second * quarter, quarter)
        for tail in reversed(tails(0)):
            if tail[0] == f:
                half_copy(0, tail).start()
    for f in (1, 0):
        second = 1 - mine[1] if f else mine[1]
        product(mine[0] * 2 * quarter + second * quarter, quarter)

    for d in range(1, nu):
        cc_copy(d).wait_recv()
    counts = cc_out[...]
    for d in range(1, nu):
        counts = counts + cc_in[d - 1]
    scaling = step_ref[1] / (BLK * (1.0 + counts))
    for i in range(ib):
        scale[i * BLK : (i + 1) * BLK, :] = jnp.broadcast_to(scaling[i : i + 1], (BLK, k))

    for level in range(levels):
        for tail in reversed(tails(level)):
            half_copy(level, tail).wait_recv()
            rows = held(level, tail)
            summed = acc[rows, :] + halves[place(level, tail)]
            if tail:
                acc[rows, :] = summed
                if tail[0]:
                    half_copy(level + 1, tail[1:]).start()
            else:
                oi_ref[rows, :] = q_ref[rows, :] + summed * scale[rows, :]

    for level in reversed(range(levels)):
        double_copy(level, (0,) * (levels - level - 1)).start()
    for level in reversed(range(levels)):
        for tail in tails(level):
            double_copy(level, tail).wait_recv()
            for lower in reversed(range(level)):
                middle = (0,) * (level - lower - 1)
                double_copy(lower, middle + (1,) + tail).start()

    for level in range(levels):
        for tail in tails(level):
            half_copy(level, tail).wait_send()
            double_copy(level, tail).wait_send()
    for d in range(1, nu):
        cc_copy(d).wait_send()

    @pl.loop(0, 2 * h)
    def _(c):
        @pl.when(z > 0)
        def _():
            rs_copy(c, left).wait_send()
            ag_copy(c + 2 * h, left).wait_send()

        @pl.when(z < ni - 1)
        def _():
            rs_copy(c + 2 * h, right).wait_send()
            ag_copy(c, right).wait_send()


def solution(mesh):
    nu, ni = mesh.shape["user"], mesh.shape["item"]

    def body(ratings, presence, user_factors, item_factors, step_sizes):
        users, items = ratings.shape
        k = item_factors.shape[1]
        ub, ib = users // BLK, items // BLK
        ibp = -(-ib // 8) * 8
        sub = -(-(BLK + k // 2 + 8) // 16) * 8
        vm = pl.BlockSpec(memory_space=pltpu.VMEM)
        hbm = pl.BlockSpec(memory_space=pltpu.HBM)
        dma = pltpu.SemaphoreType.DMA
        new_users, new_items = pl.pallas_call(
            functools.partial(kernel, nu, ni),
            out_shape=(
                pltpu.VMEM((2 * ub, BLK // 2, k), f32),
                pltpu.VMEM((items, k), f32),
            ),
            in_specs=[hbm] * 5,
            out_specs=(vm, vm),
            scratch_shapes=[
                pltpu.VMEM((ub, BLK, items), bf16),
                pltpu.SMEM((ub, ib), jnp.int32),
                pltpu.VMEM((ub, BLK, k), f32),
                pltpu.VMEM((items, k), f32),
                pltpu.SMEM((2,), f32),
                pltpu.VMEM((items, 2 * k), bf16),
                pltpu.VMEM((ib, k, k), f32),
                pltpu.VMEM((users, items), bf16),
                pltpu.VMEM((-(-ub // 16) * 8, items), f32),
                pltpu.VMEM((2 * ub, sub, k), f32),
                pltpu.VMEM((2 * ub, sub, k), f32),
                pltpu.VMEM((2 * k, users), bf16),
                pltpu.VMEM((ib, k, k), f32),
                pltpu.VMEM((items, k), f32),
                pltpu.VMEM((items, k), f32),
                pltpu.VMEM((ibp, k), f32),
                pltpu.VMEM((nu - 1, ibp, k), f32),
                pltpu.VMEM((nu - 1, items // nu, k), f32),
                dma((4,)),
                dma((ub,)),
                dma((2 * ub,)),
                dma((2 * ub,)),
                dma((2 * ub,)),
                dma((2 * ub,)),
                dma((nu - 1,)),
                dma((nu - 1,)),
                dma((nu - 1,)),
                dma((nu - 1,)),
                dma((nu - 1,)),
                dma((nu - 1,)),
            ],
            compiler_params=pltpu.CompilerParams(
                collective_id=0, has_side_effects=True, vmem_limit_bytes=56 * 2**20
            ),
            cost_estimate=pl.CostEstimate(
                flops=8 * users * items * k, bytes_accessed=2 * users * items, transcendentals=0
            ),
        )(ratings, presence, user_factors.reshape(ub, BLK, k), item_factors, step_sizes)
        return new_users.reshape(users, k), new_items

    return jax.shard_map(
        body,
        mesh=mesh,
        in_specs=(P("user", "item"), P("user", "item"), P("user", None), P("item", None), P()),
        out_specs=(P("user", None), P("item", None)),
        check_vma=False,
    )
```

```python
import functools
import itertools

import jax
import jax.numpy as jnp
from jax import lax
from jax.experimental import pallas as pl
from jax.experimental.pallas import tpu as pltpu
from jax.sharding import PartitionSpec as P

BLK = 128
LAG = 3
f32 = jnp.float32
bf16 = jnp.bfloat16
MESH = pl.DeviceIdType.MESH


def split(x):
    hi = x.astype(bf16)
    lo = (x - hi.astype(f32)).astype(bf16)
    return hi, lo


def both(x):
    return jnp.concatenate(split(x), axis=1)


def fold(x):
    k = x.shape[1] // 2
    return x[:, :k] + x[:, k:]


def three(x):
    hi, lo = split(x)
    return jnp.concatenate([hi, hi, lo], axis=0)


def stacked(x):
    return jnp.concatenate(split(x.T), axis=0)


def gram(stack, pair):
    full = jnp.dot(stack, pair, preferred_element_type=f32)
    k = full.shape[0] // 2
    full = full[:k] + full[k:]
    return full[:, :k] + full[:, k:]


def grid_of(rows, k):
    row = lax.broadcasted_iota(jnp.int32, (rows, k), 0)
    lane = lax.broadcasted_iota(jnp.int32, (rows, k), 1)
    return row, lane


def pack(g):
    k = g.shape[0]
    n = k // 2
    row, lane = grid_of(n, k)
    low = g[n:]
    packed = jnp.where(lane < row, pltpu.roll(low, n, 1), g[:n])
    diagonal = jnp.sum(jnp.where(lane == row + n, low, 0.0), axis=0, keepdims=True)
    return packed, diagonal


def unpack(packed, diagonal):
    n, k = packed.shape
    row, lane = grid_of(n, k)
    upper = jnp.where(lane > row, packed, 0.0)
    lower = pltpu.roll(jnp.where(lane < row, packed, 0.0), n, 1)
    once = jnp.concatenate([upper, lower], axis=0)
    top = jnp.where(lane == row, packed, 0.0)
    bottom = jnp.where(lane == row + n, diagonal, 0.0)
    return once + once.T + jnp.concatenate([top, bottom], axis=0)


def kernel(
    nu,
    ni,
    r_hbm,
    p_hbm,
    u_hbm,
    q_hbm,
    step_hbm,
    ou_ref,
    oi_ref,
    r_ref,
    p_ref,
    u_ref,
    q_ref,
    step_ref,
    qq,
    qg,
    masked,
    mask_row,
    gpart,
    g_in,
    apart,
    a_in,
    g_three,
    g_scale,
    ppt,
    hs,
    acc,
    scale,
    cc_out,
    cc_in,
    halves,
    *rest,
):
    levels = nu.bit_length() - 1
    (in_s, row_s, gs_s, gs_r, rs_s, rs_r, ag_s, ag_r, cc_s, cc_r, hv_s, hv_r, db_s, db_r) = rest
    ub, k = gpart.shape[0], gpart.shape[2]
    items = q_ref.shape[0]
    ib = items // BLK
    h = ub // 2
    half = BLK // 2
    kh = k // 2
    u = lax.axis_index("user")
    z = lax.axis_index("item")

    inputs = [
        pltpu.make_async_copy(src, dst, in_s.at[n])
        for n, (src, dst) in enumerate(
            ((q_hbm, q_ref), (p_hbm, p_ref), (step_hbm, step_ref), (u_hbm, u_ref))
        )
    ]
    for copy in inputs:
        copy.start()

    def fetch(b):
        rows = pl.ds(pl.multiple_of(b * BLK, BLK), BLK)
        return pltpu.make_async_copy(r_hbm.at[rows], r_ref.at[b], row_s.at[b])

    late = z // ((ni + 1) // 2)

    def ordered(m):
        return lax.rem(m + (1 - late) * h, ub)

    for m in range(ub):
        fetch(ordered(m)).start()

    barrier = pltpu.get_barrier_semaphore()
    for d in range(1, nu):
        pl.semaphore_signal(barrier, inc=1, device_id=(lax.rem(u + d, nu), z), device_id_type=MESH)

    @pl.when(z > 0)
    def _():
        pl.semaphore_signal(barrier, inc=1, device_id=(u, z - 1), device_id_type=MESH)

    @pl.when(z < ni - 1)
    def _():
        pl.semaphore_signal(barrier, inc=1, device_id=(u, z + 1), device_id_type=MESH)

    def g_copy(b, to):
        return pltpu.make_async_remote_copy(
            src_ref=gpart.at[b],
            dst_ref=g_in.at[b],
            send_sem=gs_s.at[b],
            recv_sem=gs_r.at[b],
            device_id=(u, to),
            device_id_type=MESH,
        )

    def a_copy(c, to):
        return pltpu.make_async_remote_copy(
            src_ref=apart.at[c],
            dst_ref=a_in.at[c],
            send_sem=rs_s.at[c],
            recv_sem=rs_r.at[c],
            device_id=(u, to),
            device_id_type=MESH,
        )

    def ag_copy(b, to):
        return pltpu.make_async_remote_copy(
            src_ref=ou_ref.at[b],
            dst_ref=ou_ref.at[b],
            send_sem=ag_s.at[b],
            recv_sem=ag_r.at[b],
            device_id=(u, to),
            device_id_type=MESH,
        )

    def cc_copy(d):
        return pltpu.make_async_remote_copy(
            src_ref=cc_out,
            dst_ref=cc_in.at[d - 1],
            send_sem=cc_s.at[d - 1],
            recv_sem=cc_r.at[d - 1],
            device_id=(lax.rem(u + d, nu), z),
            device_id_type=MESH,
        )

    left = jnp.maximum(z - 1, 0)
    right = jnp.minimum(z + 1, ni - 1)

    for copy in inputs:
        copy.wait()

    for i in range(ib):
        rows = pl.ds(i * BLK, BLK)
        own = q_ref[rows, :]
        pair = both(own)
        qq[rows, :] = pair
        qg[i] = gram(stacked(own), pair)
    hs[...] = jnp.zeros_like(hs)
    for i in range(ib):
        count = p_ref[0, i]
        for b in range(1, ub):
            count = count + p_ref[b, i]
        cc_out[pl.ds(i, 1), :] = jnp.full((1, k), count.astype(f32), f32)

    pl.semaphore_wait(barrier, nu - 1 + jnp.minimum(z, 1) + jnp.minimum(ni - 1 - z, 1))

    @pl.loop(0, 2)
    def _(m):
        base = lax.rem(m + 1 - late, 2) * h
        for n in range(h):
            b = base + n
            total = p_ref[b, 0]
            grams = jnp.zeros((k, k), f32)
            for i in range(ib):
                present = p_ref[b, i].astype(f32)
                mask_row[n : n + 1, i * BLK : (i + 1) * BLK] = jnp.full((1, BLK), present, f32)
                grams = grams + present * qg[i]
                if i:
                    total = total + p_ref[b, i]
            packed, diagonal = pack(grams)
            gpart[b, 0:kh] = packed
            gpart[b, kh : kh + 1] = diagonal
            gpart[b, kh + 1 : kh + 8] = jnp.full((7, k), total.astype(f32), f32)

        @pl.when(jnp.logical_and(z == ni - 1, base == 0))
        def _():
            for n in range(h):
                g_copy(base + n, left).start()

        @pl.when(jnp.logical_and(z == 0, base == h))
        def _():
            for n in range(h):
                g_copy(base + n, right).start()

        for n in range(h):
            fetch(base + n).wait()
        for n in range(h):
            b = base + n
            rows = pl.ds(pl.multiple_of(b * BLK, BLK), BLK)
            masked[rows, :] = r_ref[b] * mask_row[n : n + 1, :].astype(bf16)
        rows = pl.ds(pl.multiple_of(base * BLK, BLK), h * BLK)
        a = fold(jnp.dot(masked[rows, :], qq[...], preferred_element_type=f32))
        for n in range(2 * h):
            apart[2 * base + n] = a[n * half : (n + 1) * half]

        @pl.when(jnp.logical_and(z == ni - 1, base == 0))
        def _():
            for n in range(2 * h):
                a_copy(2 * base + n, left).start()

        @pl.when(jnp.logical_and(z == 0, base == h))
        def _():
            for n in range(2 * h):
                a_copy(2 * base + n, right).start()

    for d in range(1, nu):
        cc_copy(d).start()

    def prepare(b):
        g_three[b] = three(unpack(gpart[b, 0:kh], gpart[b, kh : kh + 1]))
        counted = 1.0 + gpart[b, kh + 1 : kh + 2]
        g_scale[b] = jnp.broadcast_to(step_ref[0] / (BLK * counted), (8, k))

    def finish(c):
        gs = g_three[c // 2]
        s = g_scale[c // 2, 0:1]
        a = apart[c]
        p = u_ref[c]
        for _ in range(2):
            ph, pl_ = split(p)
            ps = jnp.concatenate([ph, pl_, ph], axis=1)
            p = p + s * (a - jnp.dot(ps, gs, preferred_element_type=f32))
        ou_ref[c] = p

    def use(b):
        own = jnp.concatenate([ou_ref[2 * b], ou_ref[2 * b + 1]], axis=0)
        stack = stacked(own)
        ppt[:, pl.ds(pl.multiple_of(b * BLK, BLK), BLK)] = stack
        g = gram(stack, both(own))
        for i in range(ib):
            hs[i] = hs[i] + p_ref[b, i].astype(f32) * g

    def valid(j, away, count):
        return jnp.logical_and(away, jnp.logical_and(j >= 0, j < count))

    def g_step(j, b, frm, to, away, last):
        @pl.when(valid(j, away, h))
        def _():
            g_copy(b, frm).wait_recv()
            gpart[b] = gpart[b] + g_in[b]

            @pl.when(jnp.logical_not(last))
            def _():
                g_copy(b, to).start()

            @pl.when(last)
            def _():
                prepare(b)

    def a_step(j, c, frm, to, away, last):
        @pl.when(valid(j, away, 2 * h))
        def _():
            a_copy(c, frm).wait_recv()
            apart[c] = apart[c] + a_in[c]

            @pl.when(jnp.logical_not(last))
            def _():
                a_copy(c, to).start()

            @pl.when(last)
            def _():
                finish(c)
                ag_copy(c, frm).start()

            @pl.when(jnp.logical_and(last, j % 2 == 1))
            def _():
                use(c // 2)

    def gather_step(j, c, frm, to, away, last):
        @pl.when(valid(j, away, 2 * h))
        def _():
            ag_copy(c, frm).wait_recv()

            @pl.when(jnp.logical_not(last))
            def _():
                ag_copy(c, to).start()

    def use_step(j, c, away):
        @pl.when(jnp.logical_and(valid(j, away, 2 * h), j % 2 == 1))
        def _():
            use(c // 2)

    far = LAG * (ni - 1)
    first, end = z == 0, z == ni - 1
    inner_first, inner_end = z > 0, z < ni - 1

    def block(j):
        return jnp.clip(j, 0, h - 1)

    def low(j):
        return jnp.clip(j, 0, 2 * h - 1)

    def high(j):
        return low(j) + 2 * h

    @pl.loop(LAG, 2 * far + 3 * h)
    def _(t):
        jr = t - LAG * z
        jl = t - (far - LAG * z)
        gl = t - far - h - LAG * z
        gr = t - far - h - (far - LAG * z)
        g_step(jr, block(jr) + h, left, right, inner_first, end)
        g_step(jl, block(jl), right, left, inner_end, first)
        a_step(jr - h, high(jr - h), left, right, inner_first, end)
        a_step(jl - h, low(jl - h), right, left, inner_end, first)
        gather_step(gl, low(gl), left, right, inner_first, end)
        gather_step(gr, high(gr), right, left, inner_end, first)
        use_step(gl, low(gl), inner_first)
        use_step(gr, high(gr), inner_end)

    bits = [(u // (1 << i)) % 2 for i in range(levels)]
    partners = [u + (1 << i) * (1 - 2 * bits[i]) for i in range(levels)]
    core = bits[0]

    def pick(xs, level, which):
        if level == 0:
            return xs[0]
        one, two = xs[level], xs[levels - level]
        return one + which * (two - one)

    mine = [pick(bits, n, core) for n in range(levels)]
    theirs = [pick(bits, n, 1 - core) for n in range(levels)]
    to = [pick(partners, n, core) for n in range(levels)]
    leaf = items >> levels
    offset = [sum(1 << (levels - m - 1) for m in range(n)) for n in range(levels)]

    def tails(level):
        return list(itertools.product((0, 1), repeat=levels - level - 1))

    def place(level, tail):
        number = 0
        for f in tail:
            number = 2 * number + f
        return offset[level] + number

    def rows_of(digits):
        start = 0
        for n, d in enumerate(digits):
            start = start + d * (items >> (n + 1))
        return pl.ds(pl.multiple_of(start, 8), leaf)

    def turned(known, tail):
        ahead = known[levels - len(tail) :] if tail else []
        return [1 - d if f else d for d, f in zip(ahead, tail)]

    def sent(level, tail):
        known = mine if level else theirs
        return rows_of(mine[:level] + [1 - mine[level]] + turned(known, tail))

    def held(level, tail):
        return rows_of(mine[: level + 1] + turned(mine, tail))

    def half_copy(level, tail):
        n = place(level, tail)
        return pltpu.make_async_remote_copy(
            src_ref=acc.at[sent(level, tail)],
            dst_ref=halves.at[n],
            send_sem=hv_s.at[n],
            recv_sem=hv_r.at[n],
            device_id=(to[level], z),
            device_id_type=MESH,
        )

    def double_copy(level, tail):
        n = place(level, tail)
        rows = held(level, tail)
        return pltpu.make_async_remote_copy(
            src_ref=oi_ref.at[rows],
            dst_ref=oi_ref.at[rows],
            send_sem=db_s.at[n],
            recv_sem=db_r.at[n],
            device_id=(to[level], z),
            device_id_type=MESH,
        )

    def product(base, n):
        base = pl.multiple_of(base, BLK)
        wide = jnp.dot(ppt[...], masked[:, pl.ds(base, n)], preferred_element_type=f32)
        wide = wide[:k] + wide[k:]
        for m in range(n // BLK):
            rows = pl.ds(pl.multiple_of(base + m * BLK, BLK), BLK)
            pair = qq[rows, :]
            left_side = jnp.concatenate([pair, pair[:, :k]], axis=1)
            known = jnp.dot(left_side, three(hs[base // BLK + m]), preferred_element_type=f32)
            acc[rows, :] = wide[:, m * BLK : (m + 1) * BLK].T - known

    quarter = items // 4
    for f in (1, 0):
        second = 1 - theirs[1] if f else theirs[1]
        product((1 - mine[0]) * 2 * quarter + second * quarter, quarter)
        for tail in reversed(tails(0)):
            if tail[0] == f:
                half_copy(0, tail).start()
    for f in (1, 0):
        second = 1 - mine[1] if f else mine[1]
        product(mine[0] * 2 * quarter + second * quarter, quarter)

    for d in range(1, nu):
        cc_copy(d).wait_recv()
    counts = cc_out[...]
    for d in range(1, nu):
        counts = counts + cc_in[d - 1]
    scaling = step_ref[1] / (BLK * (1.0 + counts))
    for i in range(ib):
        scale[i * BLK : (i + 1) * BLK, :] = jnp.broadcast_to(scaling[i : i + 1], (BLK, k))

    for level in range(levels):
        for tail in reversed(tails(level)):
            half_copy(level, tail).wait_recv()
            rows = held(level, tail)
            summed = acc[rows, :] + halves[place(level, tail)]
            if tail:
                acc[rows, :] = summed
                if tail[0]:
                    half_copy(level + 1, tail[1:]).start()
            else:
                oi_ref[rows, :] = q_ref[rows, :] + summed * scale[rows, :]

    for level in reversed(range(levels)):
        double_copy(level, (0,) * (levels - level - 1)).start()
    for level in reversed(range(levels)):
        for tail in tails(level):
            double_copy(level, tail).wait_recv()
            for lower in reversed(range(level)):
                middle = (0,) * (level - lower - 1)
                double_copy(lower, middle + (1,) + tail).start()

    for level in range(levels):
        for tail in tails(level):
            half_copy(level, tail).wait_send()
            double_copy(level, tail).wait_send()
    for d in range(1, nu):
        cc_copy(d).wait_send()

    @pl.loop(0, 2 * h)
    def _(c):
        @pl.when(z > 0)
        def _():
            a_copy(c, left).wait_send()
            ag_copy(c + 2 * h, left).wait_send()

        @pl.when(z < ni - 1)
        def _():
            a_copy(c + 2 * h, right).wait_send()
            ag_copy(c, right).wait_send()

    @pl.loop(0, h)
    def _(b):
        @pl.when(z > 0)
        def _():
            g_copy(b, left).wait_send()

        @pl.when(z < ni - 1)
        def _():
            g_copy(b + h, right).wait_send()


def solution(mesh):
    nu, ni = mesh.shape["user"], mesh.shape["item"]

    def body(ratings, presence, user_factors, item_factors, step_sizes):
        users, items = ratings.shape
        k = item_factors.shape[1]
        ub, ib = users // BLK, items // BLK
        ibp = -(-ib // 8) * 8
        vm = pl.BlockSpec(memory_space=pltpu.VMEM)
        hbm = pl.BlockSpec(memory_space=pltpu.HBM)
        dma = pltpu.SemaphoreType.DMA
        new_users, new_items = pl.pallas_call(
            functools.partial(kernel, nu, ni),
            out_shape=(
                pltpu.VMEM((2 * ub, BLK // 2, k), f32),
                pltpu.VMEM((items, k), f32),
            ),
            in_specs=[hbm] * 5,
            out_specs=(vm, vm),
            scratch_shapes=[
                pltpu.VMEM((ub, BLK, items), bf16),
                pltpu.SMEM((ub, ib), jnp.int32),
                pltpu.VMEM((2 * ub, BLK // 2, k), f32),
                pltpu.VMEM((items, k), f32),
                pltpu.SMEM((2,), f32),
                pltpu.VMEM((items, 2 * k), bf16),
                pltpu.VMEM((ib, k, k), f32),
                pltpu.VMEM((users, items), bf16),
                pltpu.VMEM((-(-ub // 16) * 8, items), f32),
                pltpu.VMEM((ub, k // 2 + 8, k), f32),
                pltpu.VMEM((ub, k // 2 + 8, k), f32),
                pltpu.VMEM((2 * ub, BLK // 2, k), f32),
                pltpu.VMEM((2 * ub, BLK // 2, k), f32),
                pltpu.VMEM((ub, 3 * k, k), bf16),
                pltpu.VMEM((ub, 8, k), f32),
                pltpu.VMEM((2 * k, users), bf16),
                pltpu.VMEM((ib, k, k), f32),
                pltpu.VMEM((items, k), f32),
                pltpu.VMEM((items, k), f32),
                pltpu.VMEM((ibp, k), f32),
                pltpu.VMEM((nu - 1, ibp, k), f32),
                pltpu.VMEM((nu - 1, items // nu, k), f32),
                dma((4,)),
                dma((ub,)),
                dma((ub,)),
                dma((ub,)),
                dma((2 * ub,)),
                dma((2 * ub,)),
                dma((2 * ub,)),
                dma((2 * ub,)),
                dma((nu - 1,)),
                dma((nu - 1,)),
                dma((nu - 1,)),
                dma((nu - 1,)),
                dma((nu - 1,)),
                dma((nu - 1,)),
            ],
            compiler_params=pltpu.CompilerParams(
                collective_id=0, has_side_effects=True, vmem_limit_bytes=56 * 2**20
            ),
            cost_estimate=pl.CostEstimate(
                flops=8 * users * items * k, bytes_accessed=2 * users * items, transcendentals=0
            ),
        )(ratings, presence, user_factors.reshape(2 * ub, BLK // 2, k), item_factors, step_sizes)
        return new_users.reshape(users, k), new_items

    return jax.shard_map(
        body,
        mesh=mesh,
        in_specs=(P("user", "item"), P("user", "item"), P("user", None), P("item", None), P()),
        out_specs=(P("user", None), P("item", None)),
        check_vma=False,
    )
```

```python
import functools
import itertools

import jax
import jax.numpy as jnp
from jax import lax
from jax.experimental import pallas as pl
from jax.experimental.pallas import tpu as pltpu
from jax.sharding import PartitionSpec as P

BLK = 128
PIECES = 2
LAG = 3
f32 = jnp.float32
bf16 = jnp.bfloat16
MESH = pl.DeviceIdType.MESH


def split(x):
    hi = x.astype(bf16)
    lo = (x - hi.astype(f32)).astype(bf16)
    return hi, lo


def both(x):
    return jnp.concatenate(split(x), axis=1)


def fold(x):
    k = x.shape[1] // 2
    return x[:, :k] + x[:, k:]


def three(x):
    hi, lo = split(x)
    return jnp.concatenate([hi, hi, lo], axis=0)


def times(x, y_three):
    hi, lo = split(x)
    return jnp.dot(jnp.concatenate([hi, lo, hi], axis=1), y_three, preferred_element_type=f32)


def stacked(x):
    return jnp.concatenate(split(x.T), axis=0)


def gram(stack, pair):
    full = jnp.dot(stack, pair, preferred_element_type=f32)
    k = full.shape[0] // 2
    full = full[:k] + full[k:]
    return full[:, :k] + full[:, k:]


def grid_of(rows, k):
    row = lax.broadcasted_iota(jnp.int32, (rows, k), 0)
    lane = lax.broadcasted_iota(jnp.int32, (rows, k), 1)
    return row, lane


def pack(g):
    k = g.shape[0]
    n = k // 2
    row, lane = grid_of(n, k)
    low = g[n:]
    packed = jnp.where(lane < row, pltpu.roll(low, n, 1), g[:n])
    diagonal = jnp.sum(jnp.where(lane == row + n, low, 0.0), axis=0, keepdims=True)
    return packed, diagonal


def unpack(packed, diagonal):
    n, k = packed.shape
    row, lane = grid_of(n, k)
    upper = jnp.where(lane > row, packed, 0.0)
    lower = pltpu.roll(jnp.where(lane < row, packed, 0.0), n, 1)
    once = jnp.concatenate([upper, lower], axis=0)
    top = jnp.where(lane == row, packed, 0.0)
    bottom = jnp.where(lane == row + n, diagonal, 0.0)
    return once + once.T + jnp.concatenate([top, bottom], axis=0)


def kernel(
    nu,
    ni,
    r_hbm,
    p_hbm,
    u_hbm,
    q_hbm,
    step_hbm,
    ou_ref,
    oi_ref,
    r_ref,
    p_ref,
    u_ref,
    q_ref,
    step_ref,
    qq,
    qg,
    masked,
    mask_row,
    gpart,
    g_in,
    apart,
    a_in,
    g_three,
    g_scale,
    foreseen,
    ppt,
    hs,
    acc,
    scale,
    cc_out,
    cc_in,
    halves,
    *rest,
):
    levels = nu.bit_length() - 1
    (in_s, row_s, gs_s, gs_r, rs_s, rs_r, ag_s, ag_r, cc_s, cc_r, hv_s, hv_r, db_s, db_r) = rest
    ub, k = gpart.shape[0], gpart.shape[2]
    items = q_ref.shape[0]
    ib = items // BLK
    h = ub // 2
    piece = BLK // PIECES
    count = PIECES * h
    kh = k // 2
    u = lax.axis_index("user")
    z = lax.axis_index("item")

    inputs = [
        pltpu.make_async_copy(src, dst, in_s.at[n])
        for n, (src, dst) in enumerate(
            ((q_hbm, q_ref), (p_hbm, p_ref), (step_hbm, step_ref), (u_hbm, u_ref))
        )
    ]
    for copy in inputs:
        copy.start()

    def fetch(b):
        rows = pl.ds(pl.multiple_of(b * BLK, BLK), BLK)
        return pltpu.make_async_copy(r_hbm.at[rows], r_ref.at[b], row_s.at[b])

    late = z // ((ni + 1) // 2)

    def ordered(m):
        return lax.rem(m + (1 - late) * h, ub)

    for m in range(ub):
        fetch(ordered(m)).start()

    barrier = pltpu.get_barrier_semaphore()
    for d in range(1, nu):
        pl.semaphore_signal(barrier, inc=1, device_id=(lax.rem(u + d, nu), z), device_id_type=MESH)

    @pl.when(z > 0)
    def _():
        pl.semaphore_signal(barrier, inc=1, device_id=(u, z - 1), device_id_type=MESH)

    @pl.when(z < ni - 1)
    def _():
        pl.semaphore_signal(barrier, inc=1, device_id=(u, z + 1), device_id_type=MESH)

    def g_copy(b, to):
        return pltpu.make_async_remote_copy(
            src_ref=gpart.at[b],
            dst_ref=g_in.at[b],
            send_sem=gs_s.at[b],
            recv_sem=gs_r.at[b],
            device_id=(u, to),
            device_id_type=MESH,
        )

    def a_copy(c, to):
        return pltpu.make_async_remote_copy(
            src_ref=apart.at[c],
            dst_ref=a_in.at[c],
            send_sem=rs_s.at[c],
            recv_sem=rs_r.at[c],
            device_id=(u, to),
            device_id_type=MESH,
        )

    def ag_copy(b, to):
        return pltpu.make_async_remote_copy(
            src_ref=ou_ref.at[b],
            dst_ref=ou_ref.at[b],
            send_sem=ag_s.at[b],
            recv_sem=ag_r.at[b],
            device_id=(u, to),
            device_id_type=MESH,
        )

    def cc_copy(d):
        return pltpu.make_async_remote_copy(
            src_ref=cc_out,
            dst_ref=cc_in.at[d - 1],
            send_sem=cc_s.at[d - 1],
            recv_sem=cc_r.at[d - 1],
            device_id=(lax.rem(u + d, nu), z),
            device_id_type=MESH,
        )

    left = jnp.maximum(z - 1, 0)
    right = jnp.minimum(z + 1, ni - 1)

    for copy in inputs:
        copy.wait()

    for i in range(ib):
        rows = pl.ds(i * BLK, BLK)
        own = q_ref[rows, :]
        pair = both(own)
        qq[rows, :] = pair
        qg[i] = gram(stacked(own), pair)
    hs[...] = jnp.zeros_like(hs)
    for i in range(ib):
        present = p_ref[0, i]
        for b in range(1, ub):
            present = present + p_ref[b, i]
        cc_out[pl.ds(i, 1), :] = jnp.full((1, k), present.astype(f32), f32)

    pl.semaphore_wait(barrier, nu - 1 + jnp.minimum(z, 1) + jnp.minimum(ni - 1 - z, 1))

    @pl.loop(0, 2)
    def _(m):
        base = lax.rem(m + 1 - late, 2) * h
        for n in range(h):
            b = base + n
            total = p_ref[b, 0]
            grams = jnp.zeros((k, k), f32)
            for i in range(ib):
                present = p_ref[b, i].astype(f32)
                mask_row[n : n + 1, i * BLK : (i + 1) * BLK] = jnp.full((1, BLK), present, f32)
                grams = grams + present * qg[i]
                if i:
                    total = total + p_ref[b, i]
            packed, diagonal = pack(grams)
            gpart[b, 0:kh] = packed
            gpart[b, kh : kh + 1] = diagonal
            gpart[b, kh + 1 : kh + 8] = jnp.full((7, k), total.astype(f32), f32)

        @pl.when(jnp.logical_and(z == ni - 1, base == 0))
        def _():
            for n in range(h):
                g_copy(base + n, left).start()

        @pl.when(jnp.logical_and(z == 0, base == h))
        def _():
            for n in range(h):
                g_copy(base + n, right).start()

        for n in range(h):
            fetch(base + n).wait()
        for n in range(h):
            b = base + n
            rows = pl.ds(pl.multiple_of(b * BLK, BLK), BLK)
            masked[rows, :] = r_ref[b] * mask_row[n : n + 1, :].astype(bf16)
        rows = pl.ds(pl.multiple_of(base * BLK, BLK), h * BLK)
        a = fold(jnp.dot(masked[rows, :], qq[...], preferred_element_type=f32))
        for n in range(count):
            apart[PIECES * base + n] = a[n * piece : (n + 1) * piece]

        @pl.when(jnp.logical_and(z == ni - 1, base == 0))
        def _():
            for n in range(count):
                a_copy(PIECES * base + n, left).start()

        @pl.when(jnp.logical_and(z == 0, base == h))
        def _():
            for n in range(count):
                a_copy(PIECES * base + n, right).start()

    for d in range(1, nu):
        cc_copy(d).start()

    def prepare(b):
        g_three[b] = three(unpack(gpart[b, 0:kh], gpart[b, kh : kh + 1]))
        counted = 1.0 + gpart[b, kh + 1 : kh + 2]
        g_scale[b] = jnp.broadcast_to(step_ref[0] / (BLK * counted), (8, k))
        p = jnp.concatenate([u_ref[PIECES * b + n] for n in range(PIECES)], axis=0)
        known = times(p, g_three[b])
        for n in range(PIECES):
            foreseen[PIECES * b + n] = known[n * piece : (n + 1) * piece]

    def finish(c):
        b = c // PIECES
        s = g_scale[b, 0:1]
        d = apart[c] - foreseen[c]
        ou_ref[c] = u_ref[c] + s * (2.0 * d - s * times(d, g_three[b]))

    def use(b):
        own = jnp.concatenate([ou_ref[PIECES * b + n] for n in range(PIECES)], axis=0)
        stack = stacked(own)
        ppt[:, pl.ds(pl.multiple_of(b * BLK, BLK), BLK)] = stack
        g = gram(stack, both(own))
        for i in range(ib):
            hs[i] = hs[i] + p_ref[b, i].astype(f32) * g

    def valid(j, away, count):
        return jnp.logical_and(away, jnp.logical_and(j >= 0, j < count))

    def g_step(j, b, frm, to, away, last):
        @pl.when(valid(j, away, h))
        def _():
            g_copy(b, frm).wait_recv()
            gpart[b] = gpart[b] + g_in[b]

            @pl.when(jnp.logical_not(last))
            def _():
                g_copy(b, to).start()

            @pl.when(last)
            def _():
                prepare(b)

    def a_step(j, c, frm, to, away, last):
        @pl.when(valid(j, away, count))
        def _():
            a_copy(c, frm).wait_recv()
            apart[c] = apart[c] + a_in[c]

            @pl.when(jnp.logical_not(last))
            def _():
                a_copy(c, to).start()

            @pl.when(last)
            def _():
                finish(c)
                ag_copy(c, frm).start()

    def gather_step(j, c, frm, to, away, last):
        @pl.when(valid(j, away, count))
        def _():
            ag_copy(c, frm).wait_recv()

            @pl.when(jnp.logical_not(last))
            def _():
                ag_copy(c, to).start()

    def use_step(j, c, away):
        @pl.when(jnp.logical_and(valid(j, away, count), j % PIECES == PIECES - 1))
        def _():
            use(c // PIECES)

    far = LAG * (ni - 1)
    first, end = z == 0, z == ni - 1
    inner_first, inner_end = z > 0, z < ni - 1

    def block(j):
        return jnp.clip(j, 0, h - 1)

    def low(j):
        return jnp.clip(j, 0, count - 1)

    def high(j):
        return low(j) + count

    @pl.loop(LAG, 2 * far + h + count)
    def _(t):
        jr = t - LAG * z
        jl = t - (far - LAG * z)
        gl = t - far - h - LAG * z
        gr = t - far - h - (far - LAG * z)
        g_step(jr, block(jr) + h, left, right, inner_first, end)
        g_step(jl, block(jl), right, left, inner_end, first)
        a_step(jr - h, high(jr - h), left, right, inner_first, end)
        a_step(jl - h, low(jl - h), right, left, inner_end, first)
        gather_step(gl, low(gl), left, right, inner_first, end)
        gather_step(gr, high(gr), right, left, inner_end, first)
        use_step(gl, low(gl), inner_first)
        use_step(gr, high(gr), inner_end)
        late_use = t - far - h - count

        @pl.when(valid(late_use, first, h))
        def _():
            use(block(late_use))

        @pl.when(valid(late_use, end, h))
        def _():
            use(block(late_use) + h)

    bits = [(u // (1 << i)) % 2 for i in range(levels)]
    partners = [u + (1 << i) * (1 - 2 * bits[i]) for i in range(levels)]
    core = bits[0]

    def pick(xs, level, which):
        if level == 0:
            return xs[0]
        one, two = xs[level], xs[levels - level]
        return one + which * (two - one)

    mine = [pick(bits, n, core) for n in range(levels)]
    theirs = [pick(bits, n, 1 - core) for n in range(levels)]
    to = [pick(partners, n, core) for n in range(levels)]
    leaf = items >> levels
    offset = [sum(1 << (levels - m - 1) for m in range(n)) for n in range(levels)]

    def tails(level):
        return list(itertools.product((0, 1), repeat=levels - level - 1))

    def place(level, tail):
        number = 0
        for f in tail:
            number = 2 * number + f
        return offset[level] + number

    def rows_of(digits):
        start = 0
        for n, d in enumerate(digits):
            start = start + d * (items >> (n + 1))
        return pl.ds(pl.multiple_of(start, 8), leaf)

    def turned(known, tail):
        ahead = known[levels - len(tail) :] if tail else []
        return [1 - d if f else d for d, f in zip(ahead, tail)]

    def sent(level, tail):
        known = mine if level else theirs
        return rows_of(mine[:level] + [1 - mine[level]] + turned(known, tail))

    def held(level, tail):
        return rows_of(mine[: level + 1] + turned(mine, tail))

    def half_copy(level, tail):
        n = place(level, tail)
        return pltpu.make_async_remote_copy(
            src_ref=acc.at[sent(level, tail)],
            dst_ref=halves.at[n],
            send_sem=hv_s.at[n],
            recv_sem=hv_r.at[n],
            device_id=(to[level], z),
            device_id_type=MESH,
        )

    def double_copy(level, tail):
        n = place(level, tail)
        rows = held(level, tail)
        return pltpu.make_async_remote_copy(
            src_ref=oi_ref.at[rows],
            dst_ref=oi_ref.at[rows],
            send_sem=db_s.at[n],
            recv_sem=db_r.at[n],
            device_id=(to[level], z),
            device_id_type=MESH,
        )

    def product(base, n):
        base = pl.multiple_of(base, BLK)
        wide = jnp.dot(ppt[...], masked[:, pl.ds(base, n)], preferred_element_type=f32)
        wide = wide[:k] + wide[k:]
        for m in range(n // BLK):
            rows = pl.ds(pl.multiple_of(base + m * BLK, BLK), BLK)
            pair = qq[rows, :]
            left_side = jnp.concatenate([pair, pair[:, :k]], axis=1)
            known = jnp.dot(left_side, three(hs[base // BLK + m]), preferred_element_type=f32)
            acc[rows, :] = wide[:, m * BLK : (m + 1) * BLK].T - known

    quarter = items // 4
    for f in (1, 0):
        second = 1 - theirs[1] if f else theirs[1]
        product((1 - mine[0]) * 2 * quarter + second * quarter, quarter)
        for tail in reversed(tails(0)):
            if tail[0] == f:
                half_copy(0, tail).start()
    for f in (1, 0):
        second = 1 - mine[1] if f else mine[1]
        product(mine[0] * 2 * quarter + second * quarter, quarter)

    for d in range(1, nu):
        cc_copy(d).wait_recv()
    counts = cc_out[...]
    for d in range(1, nu):
        counts = counts + cc_in[d - 1]
    scaling = step_ref[1] / (BLK * (1.0 + counts))
    for i in range(ib):
        scale[i * BLK : (i + 1) * BLK, :] = jnp.broadcast_to(scaling[i : i + 1], (BLK, k))

    for level in range(levels):
        for tail in reversed(tails(level)):
            half_copy(level, tail).wait_recv()
            rows = held(level, tail)
            summed = acc[rows, :] + halves[place(level, tail)]
            if tail:
                acc[rows, :] = summed
                if tail[0]:
                    half_copy(level + 1, tail[1:]).start()
            else:
                oi_ref[rows, :] = q_ref[rows, :] + summed * scale[rows, :]

    for level in reversed(range(levels)):
        double_copy(level, (0,) * (levels - level - 1)).start()
    for level in reversed(range(levels)):
        for tail in tails(level):
            double_copy(level, tail).wait_recv()
            for lower in reversed(range(level)):
                middle = (0,) * (level - lower - 1)
                double_copy(lower, middle + (1,) + tail).start()

    for level in range(levels):
        for tail in tails(level):
            half_copy(level, tail).wait_send()
            double_copy(level, tail).wait_send()
    for d in range(1, nu):
        cc_copy(d).wait_send()

    @pl.loop(0, count)
    def _(c):
        @pl.when(z > 0)
        def _():
            a_copy(c, left).wait_send()
            ag_copy(c + count, left).wait_send()

        @pl.when(z < ni - 1)
        def _():
            a_copy(c + count, right).wait_send()
            ag_copy(c, right).wait_send()

    @pl.loop(0, h)
    def _(b):
        @pl.when(z > 0)
        def _():
            g_copy(b, left).wait_send()

        @pl.when(z < ni - 1)
        def _():
            g_copy(b + h, right).wait_send()


def solution(mesh):
    nu, ni = mesh.shape["user"], mesh.shape["item"]

    def body(ratings, presence, user_factors, item_factors, step_sizes):
        users, items = ratings.shape
        k = item_factors.shape[1]
        ub, ib = users // BLK, items // BLK
        ibp = -(-ib // 8) * 8
        vm = pl.BlockSpec(memory_space=pltpu.VMEM)
        hbm = pl.BlockSpec(memory_space=pltpu.HBM)
        dma = pltpu.SemaphoreType.DMA
        new_users, new_items = pl.pallas_call(
            functools.partial(kernel, nu, ni),
            out_shape=(
                pltpu.VMEM((PIECES * ub, BLK // PIECES, k), f32),
                pltpu.VMEM((items, k), f32),
            ),
            in_specs=[hbm] * 5,
            out_specs=(vm, vm),
            scratch_shapes=[
                pltpu.VMEM((ub, BLK, items), bf16),
                pltpu.SMEM((ub, ib), jnp.int32),
                pltpu.VMEM((PIECES * ub, BLK // PIECES, k), f32),
                pltpu.VMEM((items, k), f32),
                pltpu.SMEM((2,), f32),
                pltpu.VMEM((items, 2 * k), bf16),
                pltpu.VMEM((ib, k, k), f32),
                pltpu.VMEM((users, items), bf16),
                pltpu.VMEM((-(-ub // 16) * 8, items), f32),
                pltpu.VMEM((ub, k // 2 + 8, k), f32),
                pltpu.VMEM((ub, k // 2 + 8, k), f32),
                pltpu.VMEM((PIECES * ub, BLK // PIECES, k), f32),
                pltpu.VMEM((PIECES * ub, BLK // PIECES, k), f32),
                pltpu.VMEM((ub, 3 * k, k), bf16),
                pltpu.VMEM((ub, 8, k), f32),
                pltpu.VMEM((PIECES * ub, BLK // PIECES, k), f32),
                pltpu.VMEM((2 * k, users), bf16),
                pltpu.VMEM((ib, k, k), f32),
                pltpu.VMEM((items, k), f32),
                pltpu.VMEM((items, k), f32),
                pltpu.VMEM((ibp, k), f32),
                pltpu.VMEM((nu - 1, ibp, k), f32),
                pltpu.VMEM((nu - 1, items // nu, k), f32),
                dma((4,)),
                dma((ub,)),
                dma((ub,)),
                dma((ub,)),
                dma((PIECES * ub,)),
                dma((PIECES * ub,)),
                dma((PIECES * ub,)),
                dma((PIECES * ub,)),
                dma((nu - 1,)),
                dma((nu - 1,)),
                dma((nu - 1,)),
                dma((nu - 1,)),
                dma((nu - 1,)),
                dma((nu - 1,)),
            ],
            compiler_params=pltpu.CompilerParams(
                collective_id=0, has_side_effects=True, vmem_limit_bytes=56 * 2**20
            ),
            cost_estimate=pl.CostEstimate(
                flops=8 * users * items * k, bytes_accessed=2 * users * items, transcendentals=0
            ),
        )(ratings, presence, user_factors.reshape(PIECES * ub, BLK // PIECES, k), item_factors, step_sizes)
        return new_users.reshape(users, k), new_items

    return jax.shard_map(
        body,
        mesh=mesh,
        in_specs=(P("user", "item"), P("user", "item"), P("user", None), P("item", None), P()),
        out_specs=(P("user", None), P("item", None)),
        check_vma=False,
    )
```

```python
import functools
import itertools

import jax
import jax.numpy as jnp
from jax import lax
from jax.experimental import pallas as pl
from jax.experimental.pallas import tpu as pltpu
from jax.sharding import PartitionSpec as P

BLK = 128
PIECES = 2
LAG = 3
f32 = jnp.float32
bf16 = jnp.bfloat16
MESH = pl.DeviceIdType.MESH


def split(x):
    hi = x.astype(bf16)
    lo = (x - hi.astype(f32)).astype(bf16)
    return hi, lo


def both(x):
    return jnp.concatenate(split(x), axis=1)


def fold(x):
    k = x.shape[1] // 2
    return x[:, :k] + x[:, k:]


def three(x):
    hi, lo = split(x)
    return jnp.concatenate([hi, hi, lo], axis=0)


def times(x, y_three):
    hi, lo = split(x)
    return jnp.dot(jnp.concatenate([hi, lo, hi], axis=1), y_three, preferred_element_type=f32)


def stacked(x):
    return jnp.concatenate(split(x.T), axis=0)


def gram(stack, pair):
    full = jnp.dot(stack, pair, preferred_element_type=f32)
    k = full.shape[0] // 2
    full = full[:k] + full[k:]
    return full[:, :k] + full[:, k:]


def grid_of(rows, k):
    row = lax.broadcasted_iota(jnp.int32, (rows, k), 0)
    lane = lax.broadcasted_iota(jnp.int32, (rows, k), 1)
    return row, lane


def pack(g):
    k = g.shape[0]
    n = k // 2
    row, lane = grid_of(n, k)
    low = g[n:]
    packed = jnp.where(lane < row, pltpu.roll(low, n, 1), g[:n])
    diagonal = jnp.sum(jnp.where(lane == row + n, low, 0.0), axis=0, keepdims=True)
    return packed, diagonal


def unpack(packed, diagonal):
    n, k = packed.shape
    row, lane = grid_of(n, k)
    upper = jnp.where(lane > row, packed, 0.0)
    lower = pltpu.roll(jnp.where(lane < row, packed, 0.0), n, 1)
    once = jnp.concatenate([upper, lower], axis=0)
    top = jnp.where(lane == row, packed, 0.0)
    bottom = jnp.where(lane == row + n, diagonal, 0.0)
    return once + once.T + jnp.concatenate([top, bottom], axis=0)


def kernel(
    nu,
    ni,
    r_hbm,
    p_hbm,
    u_hbm,
    q_hbm,
    step_hbm,
    ou_ref,
    oi_ref,
    r_ref,
    p_ref,
    u_ref,
    q_ref,
    step_ref,
    qq,
    qg,
    masked,
    mask_row,
    gpart,
    g_in,
    apart,
    a_in,
    g_three,
    g_scale,
    foreseen,
    ppt,
    hs,
    acc,
    scale,
    cc_out,
    cc_in,
    halves,
    *rest,
):
    levels = nu.bit_length() - 1
    (in_s, row_s, gs_s, gs_r, rs_s, rs_r, ag_s, ag_r, cc_s, cc_r, hv_s, hv_r, db_s, db_r) = rest
    ub, k = gpart.shape[0], gpart.shape[2]
    items = q_ref.shape[0]
    ib = items // BLK
    h = ub // 2
    piece = BLK // PIECES
    count = PIECES * h
    kh = k // 2
    u = lax.axis_index("user")
    z = lax.axis_index("item")

    inputs = [
        pltpu.make_async_copy(src, dst, in_s.at[n])
        for n, (src, dst) in enumerate(
            ((q_hbm, q_ref), (p_hbm, p_ref), (step_hbm, step_ref), (u_hbm, u_ref))
        )
    ]
    for copy in inputs:
        copy.start()

    def fetch(b):
        rows = pl.ds(pl.multiple_of(b * BLK, BLK), BLK)
        return pltpu.make_async_copy(r_hbm.at[rows], r_ref.at[b], row_s.at[b])

    late = z // ((ni + 1) // 2)

    def ordered(m):
        return lax.rem(m + (1 - late) * h, ub)

    for m in range(ub):
        fetch(ordered(m)).start()

    barrier = pltpu.get_barrier_semaphore()
    for d in range(1, nu):
        pl.semaphore_signal(barrier, inc=1, device_id=(lax.rem(u + d, nu), z), device_id_type=MESH)

    @pl.when(z > 0)
    def _():
        pl.semaphore_signal(barrier, inc=1, device_id=(u, z - 1), device_id_type=MESH)

    @pl.when(z < ni - 1)
    def _():
        pl.semaphore_signal(barrier, inc=1, device_id=(u, z + 1), device_id_type=MESH)

    def g_copy(b, to):
        return pltpu.make_async_remote_copy(
            src_ref=gpart.at[b],
            dst_ref=g_in.at[b],
            send_sem=gs_s.at[b],
            recv_sem=gs_r.at[b],
            device_id=(u, to),
            device_id_type=MESH,
        )

    def a_copy(c, to):
        return pltpu.make_async_remote_copy(
            src_ref=apart.at[c],
            dst_ref=a_in.at[c],
            send_sem=rs_s.at[c],
            recv_sem=rs_r.at[c],
            device_id=(u, to),
            device_id_type=MESH,
        )

    def ag_copy(b, to):
        return pltpu.make_async_remote_copy(
            src_ref=ou_ref.at[b],
            dst_ref=ou_ref.at[b],
            send_sem=ag_s.at[b],
            recv_sem=ag_r.at[b],
            device_id=(u, to),
            device_id_type=MESH,
        )

    def cc_copy(d):
        return pltpu.make_async_remote_copy(
            src_ref=cc_out,
            dst_ref=cc_in.at[d - 1],
            send_sem=cc_s.at[d - 1],
            recv_sem=cc_r.at[d - 1],
            device_id=(lax.rem(u + d, nu), z),
            device_id_type=MESH,
        )

    left = jnp.maximum(z - 1, 0)
    right = jnp.minimum(z + 1, ni - 1)

    for copy in inputs:
        copy.wait()

    for i in range(ib):
        rows = pl.ds(i * BLK, BLK)
        own = q_ref[rows, :]
        pair = both(own)
        qq[rows, :] = pair
        qg[i] = gram(stacked(own), pair)
    hs[...] = jnp.zeros_like(hs)
    for i in range(ib):
        present = p_ref[0, i]
        for b in range(1, ub):
            present = present + p_ref[b, i]
        cc_out[pl.ds(i, 1), :] = jnp.full((1, k), present.astype(f32), f32)

    pl.semaphore_wait(barrier, nu - 1 + jnp.minimum(z, 1) + jnp.minimum(ni - 1 - z, 1))

    @pl.loop(0, 2)
    def _(m):
        base = lax.rem(m + 1 - late, 2) * h
        for n in range(h):
            b = base + n
            total = p_ref[b, 0]
            grams = jnp.zeros((k, k), f32)
            for i in range(ib):
                present = p_ref[b, i].astype(f32)
                mask_row[n : n + 1, i * BLK : (i + 1) * BLK] = jnp.full((1, BLK), present, f32)
                grams = grams + present * qg[i]
                if i:
                    total = total + p_ref[b, i]
            packed, diagonal = pack(grams)
            gpart[b, 0:kh] = packed
            gpart[b, kh : kh + 1] = diagonal
            gpart[b, kh + 1 : kh + 8] = jnp.full((7, k), total.astype(f32), f32)

        @pl.when(jnp.logical_and(z == ni - 1, base == 0))
        def _():
            for n in range(h):
                g_copy(base + n, left).start()

        @pl.when(jnp.logical_and(z == 0, base == h))
        def _():
            for n in range(h):
                g_copy(base + n, right).start()

        for n in range(h):
            fetch(base + n).wait()
        for n in range(h):
            b = base + n
            rows = pl.ds(pl.multiple_of(b * BLK, BLK), BLK)
            masked[rows, :] = r_ref[b] * mask_row[n : n + 1, :].astype(bf16)
        rows = pl.ds(pl.multiple_of(base * BLK, BLK), h * BLK)
        a = fold(jnp.dot(masked[rows, :], qq[...], preferred_element_type=f32))
        for n in range(count):
            apart[PIECES * base + n] = a[n * piece : (n + 1) * piece]

        @pl.when(jnp.logical_and(z == ni - 1, base == 0))
        def _():
            for n in range(count):
                a_copy(PIECES * base + n, left).start()

        @pl.when(jnp.logical_and(z == 0, base == h))
        def _():
            for n in range(count):
                a_copy(PIECES * base + n, right).start()

    for d in range(1, nu):
        cc_copy(d).start()

    def prepare(b):
        g_three[b] = three(unpack(gpart[b, 0:kh], gpart[b, kh : kh + 1]))
        counted = 1.0 + gpart[b, kh + 1 : kh + 2]
        g_scale[b] = jnp.broadcast_to(step_ref[0] / (BLK * counted), (8, k))
        p = jnp.concatenate([u_ref[PIECES * b + n] for n in range(PIECES)], axis=0)
        known = times(p, g_three[b])
        for n in range(PIECES):
            foreseen[PIECES * b + n] = known[n * piece : (n + 1) * piece]

    def finish(c):
        b = c // PIECES
        s = g_scale[b, 0:1]
        d = apart[c] - foreseen[c]
        ou_ref[c] = u_ref[c] + s * (2.0 * d - s * times(d, g_three[b]))

    def use(b):
        own = jnp.concatenate([ou_ref[PIECES * b + n] for n in range(PIECES)], axis=0)
        stack = stacked(own)
        ppt[:, pl.ds(pl.multiple_of(b * BLK, BLK), BLK)] = stack
        g = gram(stack, both(own))
        for i in range(ib):
            hs[i] = hs[i] + p_ref[b, i].astype(f32) * g

    def valid(j, away, count):
        return jnp.logical_and(away, jnp.logical_and(j >= 0, j < count))

    def g_step(b, frm, to, last):
        g_copy(b, frm).wait_recv()
        gpart[b] = gpart[b] + g_in[b]

        @pl.when(jnp.logical_not(last))
        def _():
            g_copy(b, to).start()

        @pl.when(last)
        def _():
            prepare(b)

    def a_step(c, frm, to, last):
        a_copy(c, frm).wait_recv()
        apart[c] = apart[c] + a_in[c]

        @pl.when(jnp.logical_not(last))
        def _():
            a_copy(c, to).start()

        @pl.when(last)
        def _():
            finish(c)
            ag_copy(c, frm).start()

    def reduce_step(j, base, frm, to, away, last):
        @pl.when(valid(j, away, h + count))
        def _():
            @pl.when(j < h)
            def _():
                g_step(jnp.clip(j, 0, h - 1) + base * h, frm, to, last)

            @pl.when(j >= h)
            def _():
                a_step(low(j - h) + base * count, frm, to, last)

    def gather_step(j, c, frm, to, away, last):
        @pl.when(valid(j, away, count))
        def _():
            ag_copy(c, frm).wait_recv()

            @pl.when(jnp.logical_not(last))
            def _():
                ag_copy(c, to).start()

    def use_step(j, c, away):
        @pl.when(jnp.logical_and(valid(j, away, count), j % PIECES == PIECES - 1))
        def _():
            use(c // PIECES)

    far = LAG * (ni - 1)
    first, end = z == 0, z == ni - 1
    inner_first, inner_end = z > 0, z < ni - 1

    def low(j):
        return jnp.clip(j, 0, count - 1)

    def high(j):
        return low(j) + count

    @pl.loop(LAG, far + h + count)
    def _(t):
        reduce_step(t - LAG * z, 1, left, right, inner_first, end)
        reduce_step(t - (far - LAG * z), 0, right, left, inner_end, first)

    @pl.when(jnp.logical_or(first, end))
    def _():
        @pl.loop(0, h)
        def _(n):
            use(n + jnp.minimum(z, 1) * h)

    for d in range(1, nu):
        cc_copy(d).wait_recv()
    counts = cc_out[...]
    for d in range(1, nu):
        counts = counts + cc_in[d - 1]
    scaling = step_ref[1] / (BLK * (1.0 + counts))
    for i in range(ib):
        scale[i * BLK : (i + 1) * BLK, :] = jnp.broadcast_to(scaling[i : i + 1], (BLK, k))

    @pl.loop(LAG, far + count)
    def _(t):
        gl = t - LAG * z
        gr = t - (far - LAG * z)
        gather_step(gl, low(gl), left, right, inner_first, end)
        gather_step(gr, high(gr), right, left, inner_end, first)
        use_step(gl, low(gl), inner_first)
        use_step(gr, high(gr), inner_end)

    bits = [(u // (1 << i)) % 2 for i in range(levels)]
    partners = [u + (1 << i) * (1 - 2 * bits[i]) for i in range(levels)]
    core = bits[0]

    def pick(xs, level, which):
        if level == 0:
            return xs[0]
        one, two = xs[level], xs[levels - level]
        return one + which * (two - one)

    mine = [pick(bits, n, core) for n in range(levels)]
    theirs = [pick(bits, n, 1 - core) for n in range(levels)]
    to = [pick(partners, n, core) for n in range(levels)]
    leaf = items >> levels
    offset = [sum(1 << (levels - m - 1) for m in range(n)) for n in range(levels)]

    def tails(level):
        return list(itertools.product((0, 1), repeat=levels - level - 1))

    def place(level, tail):
        number = 0
        for f in tail:
            number = 2 * number + f
        return offset[level] + number

    def rows_of(digits):
        start = 0
        for n, d in enumerate(digits):
            start = start + d * (items >> (n + 1))
        return pl.ds(pl.multiple_of(start, 8), leaf)

    def turned(known, tail):
        ahead = known[levels - len(tail) :] if tail else []
        return [1 - d if f else d for d, f in zip(ahead, tail)]

    def sent(level, tail):
        known = mine if level else theirs
        return rows_of(mine[:level] + [1 - mine[level]] + turned(known, tail))

    def held(level, tail):
        return rows_of(mine[: level + 1] + turned(mine, tail))

    def half_copy(level, tail):
        n = place(level, tail)
        return pltpu.make_async_remote_copy(
            src_ref=acc.at[sent(level, tail)],
            dst_ref=halves.at[n],
            send_sem=hv_s.at[n],
            recv_sem=hv_r.at[n],
            device_id=(to[level], z),
            device_id_type=MESH,
        )

    def double_copy(level, tail):
        n = place(level, tail)
        rows = held(level, tail)
        return pltpu.make_async_remote_copy(
            src_ref=oi_ref.at[rows],
            dst_ref=oi_ref.at[rows],
            send_sem=db_s.at[n],
            recv_sem=db_r.at[n],
            device_id=(to[level], z),
            device_id_type=MESH,
        )

    def product(base, n):
        base = pl.multiple_of(base, BLK)
        wide = jnp.dot(ppt[...], masked[:, pl.ds(base, n)], preferred_element_type=f32)
        wide = wide[:k] + wide[k:]
        for m in range(n // BLK):
            rows = pl.ds(pl.multiple_of(base + m * BLK, BLK), BLK)
            pair = qq[rows, :]
            left_side = jnp.concatenate([pair, pair[:, :k]], axis=1)
            known = jnp.dot(left_side, three(hs[base // BLK + m]), preferred_element_type=f32)
            acc[rows, :] = wide[:, m * BLK : (m + 1) * BLK].T - known

    quarter = items // 4
    for f in (1, 0):
        second = 1 - theirs[1] if f else theirs[1]
        product((1 - mine[0]) * 2 * quarter + second * quarter, quarter)
        for tail in reversed(tails(0)):
            if tail[0] == f:
                half_copy(0, tail).start()
    for f in (1, 0):
        second = 1 - mine[1] if f else mine[1]
        product(mine[0] * 2 * quarter + second * quarter, quarter)

    for level in range(levels):
        for tail in reversed(tails(level)):
            half_copy(level, tail).wait_recv()
            rows = held(level, tail)
            summed = acc[rows, :] + halves[place(level, tail)]
            if tail:
                acc[rows, :] = summed
                if tail[0]:
                    half_copy(level + 1, tail[1:]).start()
            else:
                oi_ref[rows, :] = q_ref[rows, :] + summed * scale[rows, :]

    for level in reversed(range(levels)):
        double_copy(level, (0,) * (levels - level - 1)).start()
    for level in reversed(range(levels)):
        for tail in tails(level):
            double_copy(level, tail).wait_recv()
            for lower in reversed(range(level)):
                middle = (0,) * (level - lower - 1)
                double_copy(lower, middle + (1,) + tail).start()

    for level in range(levels):
        for tail in tails(level):
            half_copy(level, tail).wait_send()
            double_copy(level, tail).wait_send()
    for d in range(1, nu):
        cc_copy(d).wait_send()

    @pl.loop(0, count)
    def _(c):
        @pl.when(z > 0)
        def _():
            a_copy(c, left).wait_send()
            ag_copy(c + count, left).wait_send()

        @pl.when(z < ni - 1)
        def _():
            a_copy(c + count, right).wait_send()
            ag_copy(c, right).wait_send()

    @pl.loop(0, h)
    def _(b):
        @pl.when(z > 0)
        def _():
            g_copy(b, left).wait_send()

        @pl.when(z < ni - 1)
        def _():
            g_copy(b + h, right).wait_send()


def solution(mesh):
    nu, ni = mesh.shape["user"], mesh.shape["item"]

    def body(ratings, presence, user_factors, item_factors, step_sizes):
        users, items = ratings.shape
        k = item_factors.shape[1]
        ub, ib = users // BLK, items // BLK
        ibp = -(-ib // 8) * 8
        vm = pl.BlockSpec(memory_space=pltpu.VMEM)
        hbm = pl.BlockSpec(memory_space=pltpu.HBM)
        dma = pltpu.SemaphoreType.DMA
        new_users, new_items = pl.pallas_call(
            functools.partial(kernel, nu, ni),
            out_shape=(
                pltpu.VMEM((PIECES * ub, BLK // PIECES, k), f32),
                pltpu.VMEM((items, k), f32),
            ),
            in_specs=[hbm] * 5,
            out_specs=(vm, vm),
            scratch_shapes=[
                pltpu.VMEM((ub, BLK, items), bf16),
                pltpu.SMEM((ub, ib), jnp.int32),
                pltpu.VMEM((PIECES * ub, BLK // PIECES, k), f32),
                pltpu.VMEM((items, k), f32),
                pltpu.SMEM((2,), f32),
                pltpu.VMEM((items, 2 * k), bf16),
                pltpu.VMEM((ib, k, k), f32),
                pltpu.VMEM((users, items), bf16),
                pltpu.VMEM((-(-ub // 16) * 8, items), f32),
                pltpu.VMEM((ub, k // 2 + 8, k), f32),
                pltpu.VMEM((ub, k // 2 + 8, k), f32),
                pltpu.VMEM((PIECES * ub, BLK // PIECES, k), f32),
                pltpu.VMEM((PIECES * ub, BLK // PIECES, k), f32),
                pltpu.VMEM((ub, 3 * k, k), bf16),
                pltpu.VMEM((ub, 8, k), f32),
                pltpu.VMEM((PIECES * ub, BLK // PIECES, k), f32),
                pltpu.VMEM((2 * k, users), bf16),
                pltpu.VMEM((ib, k, k), f32),
                pltpu.VMEM((items, k), f32),
                pltpu.VMEM((items, k), f32),
                pltpu.VMEM((ibp, k), f32),
                pltpu.VMEM((nu - 1, ibp, k), f32),
                pltpu.VMEM((nu - 1, items // nu, k), f32),
                dma((4,)),
                dma((ub,)),
                dma((ub,)),
                dma((ub,)),
                dma((PIECES * ub,)),
                dma((PIECES * ub,)),
                dma((PIECES * ub,)),
                dma((PIECES * ub,)),
                dma((nu - 1,)),
                dma((nu - 1,)),
                dma((nu - 1,)),
                dma((nu - 1,)),
                dma((nu - 1,)),
                dma((nu - 1,)),
            ],
            compiler_params=pltpu.CompilerParams(
                collective_id=0, has_side_effects=True, vmem_limit_bytes=56 * 2**20
            ),
            cost_estimate=pl.CostEstimate(
                flops=8 * users * items * k, bytes_accessed=2 * users * items, transcendentals=0
            ),
        )(ratings, presence, user_factors.reshape(PIECES * ub, BLK // PIECES, k), item_factors, step_sizes)
        return new_users.reshape(users, k), new_items

    return jax.shard_map(
        body,
        mesh=mesh,
        in_specs=(P("user", "item"), P("user", "item"), P("user", None), P("item", None), P()),
        out_specs=(P("user", None), P("item", None)),
        check_vma=False,
    )
```

```python
import functools
import itertools

import jax
import jax.numpy as jnp
from jax import lax
from jax.experimental import pallas as pl
from jax.experimental.pallas import tpu as pltpu
from jax.sharding import PartitionSpec as P

BLK = 128
PIECES = 2
LAG = 3
f32 = jnp.float32
bf16 = jnp.bfloat16
MESH = pl.DeviceIdType.MESH


def split(x):
    hi = x.astype(bf16)
    lo = (x - hi.astype(f32)).astype(bf16)
    return hi, lo


def both(x):
    return jnp.concatenate(split(x), axis=1)


def fold(x):
    k = x.shape[1] // 2
    return x[:, :k] + x[:, k:]


def three(x):
    hi, lo = split(x)
    return jnp.concatenate([hi, hi, lo], axis=0)


def times(x, y_three):
    hi, lo = split(x)
    return jnp.dot(jnp.concatenate([hi, lo, hi], axis=1), y_three, preferred_element_type=f32)


def stacked(x):
    return jnp.concatenate(split(x.T), axis=0)


def gram(stack, pair):
    full = jnp.dot(stack, pair, preferred_element_type=f32)
    k = full.shape[0] // 2
    full = full[:k] + full[k:]
    return full[:, :k] + full[:, k:]


def grid_of(rows, k):
    row = lax.broadcasted_iota(jnp.int32, (rows, k), 0)
    lane = lax.broadcasted_iota(jnp.int32, (rows, k), 1)
    return row, lane


def pack(g):
    k = g.shape[0]
    n = k // 2
    row, lane = grid_of(n, k)
    low = g[n:]
    packed = jnp.where(lane < row, pltpu.roll(low, n, 1), g[:n])
    diagonal = jnp.sum(jnp.where(lane == row + n, low, 0.0), axis=0, keepdims=True)
    return packed, diagonal


def unpack(packed, diagonal):
    n, k = packed.shape
    row, lane = grid_of(n, k)
    upper = jnp.where(lane > row, packed, 0.0)
    lower = pltpu.roll(jnp.where(lane < row, packed, 0.0), n, 1)
    once = jnp.concatenate([upper, lower], axis=0)
    top = jnp.where(lane == row, packed, 0.0)
    bottom = jnp.where(lane == row + n, diagonal, 0.0)
    return once + once.T + jnp.concatenate([top, bottom], axis=0)


def kernel(
    nu,
    ni,
    r_hbm,
    p_hbm,
    u_hbm,
    q_hbm,
    step_hbm,
    ou_ref,
    oi_ref,
    r_ref,
    p_ref,
    u_ref,
    q_ref,
    step_ref,
    qq,
    qg,
    masked,
    mask_row,
    gpart,
    g_in,
    apart,
    a_in,
    g_three,
    g_scale,
    foreseen,
    ppt,
    hs,
    acc,
    scale,
    cc_out,
    cc_in,
    halves,
    *rest,
):
    levels = nu.bit_length() - 1
    (in_s, row_s, gs_s, gs_r, rs_s, rs_r, ag_s, ag_r, cc_s, cc_r, hv_s, hv_r, db_s, db_r) = rest
    ub, k = gpart.shape[0], gpart.shape[2]
    items = q_ref.shape[0]
    ib = items // BLK
    h = ub // 2
    piece = BLK // PIECES
    count = PIECES * h
    kh = k // 2
    u = lax.axis_index("user")
    z = lax.axis_index("item")

    inputs = [
        pltpu.make_async_copy(src, dst, in_s.at[n])
        for n, (src, dst) in enumerate(
            ((q_hbm, q_ref), (p_hbm, p_ref), (step_hbm, step_ref), (u_hbm, u_ref))
        )
    ]
    for copy in inputs:
        copy.start()

    def fetch(b):
        rows = pl.ds(pl.multiple_of(b * BLK, BLK), BLK)
        return pltpu.make_async_copy(r_hbm.at[rows], r_ref.at[b], row_s.at[b])

    late = z // ((ni + 1) // 2)

    def ordered(m):
        return lax.rem(m + (1 - late) * h, ub)

    for m in range(ub):
        fetch(ordered(m)).start()

    barrier = pltpu.get_barrier_semaphore()
    for d in range(1, nu):
        pl.semaphore_signal(barrier, inc=1, device_id=(lax.rem(u + d, nu), z), device_id_type=MESH)

    @pl.when(z > 0)
    def _():
        pl.semaphore_signal(barrier, inc=1, device_id=(u, z - 1), device_id_type=MESH)

    @pl.when(z < ni - 1)
    def _():
        pl.semaphore_signal(barrier, inc=1, device_id=(u, z + 1), device_id_type=MESH)

    def g_copy(b, to):
        return pltpu.make_async_remote_copy(
            src_ref=gpart.at[b],
            dst_ref=g_in.at[b],
            send_sem=gs_s.at[b],
            recv_sem=gs_r.at[b],
            device_id=(u, to),
            device_id_type=MESH,
        )

    def a_copy(c, to):
        return pltpu.make_async_remote_copy(
            src_ref=apart.at[c],
            dst_ref=a_in.at[c],
            send_sem=rs_s.at[c],
            recv_sem=rs_r.at[c],
            device_id=(u, to),
            device_id_type=MESH,
        )

    def ag_copy(b, to):
        return pltpu.make_async_remote_copy(
            src_ref=ou_ref.at[b],
            dst_ref=ou_ref.at[b],
            send_sem=ag_s.at[b],
            recv_sem=ag_r.at[b],
            device_id=(u, to),
            device_id_type=MESH,
        )

    def cc_copy(d):
        return pltpu.make_async_remote_copy(
            src_ref=cc_out,
            dst_ref=cc_in.at[d - 1],
            send_sem=cc_s.at[d - 1],
            recv_sem=cc_r.at[d - 1],
            device_id=(lax.rem(u + d, nu), z),
            device_id_type=MESH,
        )

    left = jnp.maximum(z - 1, 0)
    right = jnp.minimum(z + 1, ni - 1)

    for copy in inputs:
        copy.wait()

    for i in range(ib):
        rows = pl.ds(i * BLK, BLK)
        own = q_ref[rows, :]
        pair = both(own)
        qq[rows, :] = pair
        qg[i] = gram(stacked(own), pair)
    hs[...] = jnp.zeros_like(hs)
    for i in range(ib):
        present = p_ref[0, i]
        for b in range(1, ub):
            present = present + p_ref[b, i]
        cc_out[pl.ds(i, 1), :] = jnp.full((1, k), present.astype(f32), f32)

    pl.semaphore_wait(barrier, nu - 1 + jnp.minimum(z, 1) + jnp.minimum(ni - 1 - z, 1))

    def work_out(m):
        base = lax.rem(m + 1 - late, 2) * h
        for n in range(h):
            b = base + n
            total = p_ref[b, 0]
            grams = jnp.zeros((k, k), f32)
            for i in range(ib):
                present = p_ref[b, i].astype(f32)
                mask_row[n : n + 1, i * BLK : (i + 1) * BLK] = jnp.full((1, BLK), present, f32)
                grams = grams + present * qg[i]
                if i:
                    total = total + p_ref[b, i]
            packed, diagonal = pack(grams)
            gpart[b, 0:kh] = packed
            gpart[b, kh : kh + 1] = diagonal
            gpart[b, kh + 1 : kh + 8] = jnp.full((7, k), total.astype(f32), f32)

        @pl.when(jnp.logical_and(z == ni - 1, base == 0))
        def _():
            for n in range(h):
                g_copy(base + n, left).start()

        @pl.when(jnp.logical_and(z == 0, base == h))
        def _():
            for n in range(h):
                g_copy(base + n, right).start()

        for n in range(h):
            fetch(base + n).wait()
        for n in range(h):
            b = base + n
            rows = pl.ds(pl.multiple_of(b * BLK, BLK), BLK)
            masked[rows, :] = r_ref[b] * mask_row[n : n + 1, :].astype(bf16)
        rows = pl.ds(pl.multiple_of(base * BLK, BLK), h * BLK)
        a = fold(jnp.dot(masked[rows, :], qq[...], preferred_element_type=f32))
        for n in range(count):
            apart[PIECES * base + n] = a[n * piece : (n + 1) * piece]

        @pl.when(jnp.logical_and(z == ni - 1, base == 0))
        def _():
            for n in range(count):
                a_copy(PIECES * base + n, left).start()

        @pl.when(jnp.logical_and(z == 0, base == h))
        def _():
            for n in range(count):
                a_copy(PIECES * base + n, right).start()

    work_out(0)

    for d in range(1, nu):
        cc_copy(d).start()

    def prepare(b):
        g_three[b] = three(unpack(gpart[b, 0:kh], gpart[b, kh : kh + 1]))
        counted = 1.0 + gpart[b, kh + 1 : kh + 2]
        g_scale[b] = jnp.broadcast_to(step_ref[0] / (BLK * counted), (8, k))
        p = jnp.concatenate([u_ref[PIECES * b + n] for n in range(PIECES)], axis=0)
        known = times(p, g_three[b])
        for n in range(PIECES):
            foreseen[PIECES * b + n] = known[n * piece : (n + 1) * piece]

    def finish(c):
        b = c // PIECES
        s = g_scale[b, 0:1]
        d = apart[c] - foreseen[c]
        ou_ref[c] = u_ref[c] + s * (2.0 * d - s * times(d, g_three[b]))

    def use(b):
        own = jnp.concatenate([ou_ref[PIECES * b + n] for n in range(PIECES)], axis=0)
        stack = stacked(own)
        ppt[:, pl.ds(pl.multiple_of(b * BLK, BLK), BLK)] = stack
        g = gram(stack, both(own))
        for i in range(ib):
            hs[i] = hs[i] + p_ref[b, i].astype(f32) * g

    def valid(j, away, count):
        return jnp.logical_and(away, jnp.logical_and(j >= 0, j < count))

    def g_step(b, frm, to, last):
        g_copy(b, frm).wait_recv()
        gpart[b] = gpart[b] + g_in[b]

        @pl.when(jnp.logical_not(last))
        def _():
            g_copy(b, to).start()

        @pl.when(last)
        def _():
            prepare(b)

    def a_step(c, frm, to, last):
        a_copy(c, frm).wait_recv()
        apart[c] = apart[c] + a_in[c]

        @pl.when(jnp.logical_not(last))
        def _():
            a_copy(c, to).start()

        @pl.when(last)
        def _():
            finish(c)
            ag_copy(c, frm).start()

    def reduce_step(j, base, frm, to, away, last):
        @pl.when(valid(j, away, h + count))
        def _():
            @pl.when(j < h)
            def _():
                g_step(jnp.clip(j, 0, h - 1) + base * h, frm, to, last)

            @pl.when(j >= h)
            def _():
                a_step(low(j - h) + base * count, frm, to, last)

    def gather_step(j, c, frm, to, away, last):
        @pl.when(valid(j, away, count))
        def _():
            ag_copy(c, frm).wait_recv()

            @pl.when(jnp.logical_not(last))
            def _():
                ag_copy(c, to).start()

    def use_step(j, c, away):
        @pl.when(jnp.logical_and(valid(j, away, count), j % PIECES == PIECES - 1))
        def _():
            use(c // PIECES)

    far = LAG * (ni - 1)
    first, end = z == 0, z == ni - 1
    inner_first, inner_end = z > 0, z < ni - 1

    def low(j):
        return jnp.clip(j, 0, count - 1)

    def high(j):
        return low(j) + count

    turn = LAG * (ni // 2 - 1) + min(h, LAG) - 1
    if turn < LAG:
        work_out(1)

    @pl.loop(LAG, far + h + count)
    def _(t):
        reduce_step(t - LAG * z, 1, left, right, inner_first, end)
        reduce_step(t - (far - LAG * z), 0, right, left, inner_end, first)
        if turn >= LAG:

            @pl.when(t == turn)
            def _():
                work_out(1)

    @pl.when(jnp.logical_or(first, end))
    def _():
        @pl.loop(0, h)
        def _(n):
            use(n + jnp.minimum(z, 1) * h)

    for d in range(1, nu):
        cc_copy(d).wait_recv()
    counts = cc_out[...]
    for d in range(1, nu):
        counts = counts + cc_in[d - 1]
    scaling = step_ref[1] / (BLK * (1.0 + counts))
    for i in range(ib):
        scale[i * BLK : (i + 1) * BLK, :] = jnp.broadcast_to(scaling[i : i + 1], (BLK, k))

    @pl.loop(LAG, far + count)
    def _(t):
        gl = t - LAG * z
        gr = t - (far - LAG * z)
        gather_step(gl, low(gl), left, right, inner_first, end)
        gather_step(gr, high(gr), right, left, inner_end, first)
        use_step(gl, low(gl), inner_first)
        use_step(gr, high(gr), inner_end)

    bits = [(u // (1 << i)) % 2 for i in range(levels)]
    partners = [u + (1 << i) * (1 - 2 * bits[i]) for i in range(levels)]
    core = bits[0]

    def pick(xs, level, which):
        if level == 0:
            return xs[0]
        one, two = xs[level], xs[levels - level]
        return one + which * (two - one)

    mine = [pick(bits, n, core) for n in range(levels)]
    theirs = [pick(bits, n, 1 - core) for n in range(levels)]
    to = [pick(partners, n, core) for n in range(levels)]
    leaf = items >> levels
    offset = [sum(1 << (levels - m - 1) for m in range(n)) for n in range(levels)]

    def tails(level):
        return list(itertools.product((0, 1), repeat=levels - level - 1))

    def place(level, tail):
        number = 0
        for f in tail:
            number = 2 * number + f
        return offset[level] + number

    def rows_of(digits):
        start = 0
        for n, d in enumerate(digits):
            start = start + d * (items >> (n + 1))
        return pl.ds(pl.multiple_of(start, 8), leaf)

    def turned(known, tail):
        ahead = known[levels - len(tail) :] if tail else []
        return [1 - d if f else d for d, f in zip(ahead, tail)]

    def sent(level, tail):
        known = mine if level else theirs
        return rows_of(mine[:level] + [1 - mine[level]] + turned(known, tail))

    def held(level, tail):
        return rows_of(mine[: level + 1] + turned(mine, tail))

    def half_copy(level, tail):
        n = place(level, tail)
        return pltpu.make_async_remote_copy(
            src_ref=acc.at[sent(level, tail)],
            dst_ref=halves.at[n],
            send_sem=hv_s.at[n],
            recv_sem=hv_r.at[n],
            device_id=(to[level], z),
            device_id_type=MESH,
        )

    def double_copy(level, tail):
        n = place(level, tail)
        rows = held(level, tail)
        return pltpu.make_async_remote_copy(
            src_ref=oi_ref.at[rows],
            dst_ref=oi_ref.at[rows],
            send_sem=db_s.at[n],
            recv_sem=db_r.at[n],
            device_id=(to[level], z),
            device_id_type=MESH,
        )

    def product(base, n):
        base = pl.multiple_of(base, BLK)
        wide = jnp.dot(ppt[...], masked[:, pl.ds(base, n)], preferred_element_type=f32)
        wide = wide[:k] + wide[k:]
        for m in range(n // BLK):
            rows = pl.ds(pl.multiple_of(base + m * BLK, BLK), BLK)
            pair = qq[rows, :]
            left_side = jnp.concatenate([pair, pair[:, :k]], axis=1)
            known = jnp.dot(left_side, three(hs[base // BLK + m]), preferred_element_type=f32)
            acc[rows, :] = wide[:, m * BLK : (m + 1) * BLK].T - known

    quarter = items // 4
    for f in (1, 0):
        second = 1 - theirs[1] if f else theirs[1]
        product((1 - mine[0]) * 2 * quarter + second * quarter, quarter)
        for tail in reversed(tails(0)):
            if tail[0] == f:
                half_copy(0, tail).start()
    for level in range(levels):
        for tail in reversed(tails(level)):
            if level == 0 and all(tail[1:]):
                second = 1 - mine[1] if tail[0] else mine[1]
                product(mine[0] * 2 * quarter + second * quarter, quarter)
            half_copy(level, tail).wait_recv()
            rows = held(level, tail)
            summed = acc[rows, :] + halves[place(level, tail)]
            if tail:
                acc[rows, :] = summed
                if tail[0]:
                    half_copy(level + 1, tail[1:]).start()
            else:
                oi_ref[rows, :] = q_ref[rows, :] + summed * scale[rows, :]

    for level in reversed(range(levels)):
        double_copy(level, (0,) * (levels - level - 1)).start()
    for level in reversed(range(levels)):
        for tail in tails(level):
            double_copy(level, tail).wait_recv()
            for lower in reversed(range(level)):
                middle = (0,) * (level - lower - 1)
                double_copy(lower, middle + (1,) + tail).start()

    for level in range(levels):
        for tail in tails(level):
            half_copy(level, tail).wait_send()
            double_copy(level, tail).wait_send()
    for d in range(1, nu):
        cc_copy(d).wait_send()

    @pl.loop(0, count)
    def _(c):
        @pl.when(z > 0)
        def _():
            a_copy(c, left).wait_send()
            ag_copy(c + count, left).wait_send()

        @pl.when(z < ni - 1)
        def _():
            a_copy(c + count, right).wait_send()
            ag_copy(c, right).wait_send()

    @pl.loop(0, h)
    def _(b):
        @pl.when(z > 0)
        def _():
            g_copy(b, left).wait_send()

        @pl.when(z < ni - 1)
        def _():
            g_copy(b + h, right).wait_send()


def solution(mesh):
    nu, ni = mesh.shape["user"], mesh.shape["item"]

    def body(ratings, presence, user_factors, item_factors, step_sizes):
        users, items = ratings.shape
        k = item_factors.shape[1]
        ub, ib = users // BLK, items // BLK
        ibp = -(-ib // 8) * 8
        vm = pl.BlockSpec(memory_space=pltpu.VMEM)
        hbm = pl.BlockSpec(memory_space=pltpu.HBM)
        dma = pltpu.SemaphoreType.DMA
        new_users, new_items = pl.pallas_call(
            functools.partial(kernel, nu, ni),
            out_shape=(
                pltpu.VMEM((PIECES * ub, BLK // PIECES, k), f32),
                pltpu.VMEM((items, k), f32),
            ),
            in_specs=[hbm] * 5,
            out_specs=(vm, vm),
            scratch_shapes=[
                pltpu.VMEM((ub, BLK, items), bf16),
                pltpu.SMEM((ub, ib), jnp.int32),
                pltpu.VMEM((PIECES * ub, BLK // PIECES, k), f32),
                pltpu.VMEM((items, k), f32),
                pltpu.SMEM((2,), f32),
                pltpu.VMEM((items, 2 * k), bf16),
                pltpu.VMEM((ib, k, k), f32),
                pltpu.VMEM((users, items), bf16),
                pltpu.VMEM((-(-ub // 16) * 8, items), f32),
                pltpu.VMEM((ub, k // 2 + 8, k), f32),
                pltpu.VMEM((ub, k // 2 + 8, k), f32),
                pltpu.VMEM((PIECES * ub, BLK // PIECES, k), f32),
                pltpu.VMEM((PIECES * ub, BLK // PIECES, k), f32),
                pltpu.VMEM((ub, 3 * k, k), bf16),
                pltpu.VMEM((ub, 8, k), f32),
                pltpu.VMEM((PIECES * ub, BLK // PIECES, k), f32),
                pltpu.VMEM((2 * k, users), bf16),
                pltpu.VMEM((ib, k, k), f32),
                pltpu.VMEM((items, k), f32),
                pltpu.VMEM((items, k), f32),
                pltpu.VMEM((ibp, k), f32),
                pltpu.VMEM((nu - 1, ibp, k), f32),
                pltpu.VMEM((nu - 1, items // nu, k), f32),
                dma((4,)),
                dma((ub,)),
                dma((ub,)),
                dma((ub,)),
                dma((PIECES * ub,)),
                dma((PIECES * ub,)),
                dma((PIECES * ub,)),
                dma((PIECES * ub,)),
                dma((nu - 1,)),
                dma((nu - 1,)),
                dma((nu - 1,)),
                dma((nu - 1,)),
                dma((nu - 1,)),
                dma((nu - 1,)),
            ],
            compiler_params=pltpu.CompilerParams(
                collective_id=0, has_side_effects=True, vmem_limit_bytes=56 * 2**20
            ),
            cost_estimate=pl.CostEstimate(
                flops=8 * users * items * k, bytes_accessed=2 * users * items, transcendentals=0
            ),
        )(ratings, presence, user_factors.reshape(PIECES * ub, BLK // PIECES, k), item_factors, step_sizes)
        return new_users.reshape(users, k), new_items

    return jax.shard_map(
        body,
        mesh=mesh,
        in_specs=(P("user", "item"), P("user", "item"), P("user", None), P("item", None), P()),
        out_specs=(P("user", None), P("item", None)),
        check_vma=False,
    )
```

```python
import functools
import itertools

import jax
import jax.numpy as jnp
from jax import lax
from jax.experimental import pallas as pl
from jax.experimental.pallas import tpu as pltpu
from jax.sharding import PartitionSpec as P

BLK = 128
PIECES = 2
LAG = 5
f32 = jnp.float32
bf16 = jnp.bfloat16
MESH = pl.DeviceIdType.MESH


def split(x):
    hi = x.astype(bf16)
    lo = (x - hi.astype(f32)).astype(bf16)
    return hi, lo


def both(x):
    return jnp.concatenate(split(x), axis=1)


def fold(x):
    k = x.shape[1] // 2
    return x[:, :k] + x[:, k:]


def three(x):
    hi, lo = split(x)
    return jnp.concatenate([hi, hi, lo], axis=0)


def times(x, y_three):
    hi, lo = split(x)
    return jnp.dot(jnp.concatenate([hi, lo, hi], axis=1), y_three, preferred_element_type=f32)


def stacked(x):
    return jnp.concatenate(split(x.T), axis=0)


def gram(stack, pair):
    full = jnp.dot(stack, pair, preferred_element_type=f32)
    k = full.shape[0] // 2
    full = full[:k] + full[k:]
    return full[:, :k] + full[:, k:]


def grid_of(rows, k):
    row = lax.broadcasted_iota(jnp.int32, (rows, k), 0)
    lane = lax.broadcasted_iota(jnp.int32, (rows, k), 1)
    return row, lane


def pack(g):
    k = g.shape[0]
    n = k // 2
    row, lane = grid_of(n, k)
    low = g[n:]
    packed = jnp.where(lane < row, pltpu.roll(low, n, 1), g[:n])
    diagonal = jnp.sum(jnp.where(lane == row + n, low, 0.0), axis=0, keepdims=True)
    return packed, diagonal


def unpack(packed, diagonal):
    n, k = packed.shape
    row, lane = grid_of(n, k)
    upper = jnp.where(lane > row, packed, 0.0)
    lower = pltpu.roll(jnp.where(lane < row, packed, 0.0), n, 1)
    once = jnp.concatenate([upper, lower], axis=0)
    top = jnp.where(lane == row, packed, 0.0)
    bottom = jnp.where(lane == row + n, diagonal, 0.0)
    return once + once.T + jnp.concatenate([top, bottom], axis=0)


def kernel(
    nu,
    ni,
    r_hbm,
    p_hbm,
    u_hbm,
    q_hbm,
    step_hbm,
    ou_ref,
    oi_ref,
    r_ref,
    p_ref,
    u_ref,
    q_ref,
    step_ref,
    qq,
    qg,
    masked,
    mask_row,
    gpart,
    g_in,
    apart,
    a_in,
    g_three,
    g_scale,
    foreseen,
    ppt,
    hs,
    acc,
    scale,
    cc_out,
    cc_in,
    halves,
    *rest,
):
    levels = nu.bit_length() - 1
    (in_s, row_s, gs_s, gs_r, rs_s, rs_r, ag_s, ag_r, cc_s, cc_r, hv_s, hv_r, db_s, db_r) = rest
    ub, k = gpart.shape[0], gpart.shape[2]
    items = q_ref.shape[0]
    ib = items // BLK
    h = ub // 2
    piece = BLK // PIECES
    count = PIECES * h
    kh = k // 2
    u = lax.axis_index("user")
    z = lax.axis_index("item")

    inputs = [
        pltpu.make_async_copy(src, dst, in_s.at[n])
        for n, (src, dst) in enumerate(
            ((q_hbm, q_ref), (p_hbm, p_ref), (step_hbm, step_ref), (u_hbm, u_ref))
        )
    ]
    for copy in inputs:
        copy.start()

    def fetch(b):
        rows = pl.ds(pl.multiple_of(b * BLK, BLK), BLK)
        return pltpu.make_async_copy(r_hbm.at[rows], r_ref.at[b], row_s.at[b])

    late = z // ((ni + 1) // 2)

    def ordered(m):
        return lax.rem(m + (1 - late) * h, ub)

    for m in range(ub):
        fetch(ordered(m)).start()

    barrier = pltpu.get_barrier_semaphore()
    for d in range(1, nu):
        pl.semaphore_signal(barrier, inc=1, device_id=(lax.rem(u + d, nu), z), device_id_type=MESH)

    @pl.when(z > 0)
    def _():
        pl.semaphore_signal(barrier, inc=1, device_id=(u, z - 1), device_id_type=MESH)

    @pl.when(z < ni - 1)
    def _():
        pl.semaphore_signal(barrier, inc=1, device_id=(u, z + 1), device_id_type=MESH)

    def g_copy(b, to):
        return pltpu.make_async_remote_copy(
            src_ref=gpart.at[b],
            dst_ref=g_in.at[b],
            send_sem=gs_s.at[b],
            recv_sem=gs_r.at[b],
            device_id=(u, to),
            device_id_type=MESH,
        )

    def a_copy(c, to):
        return pltpu.make_async_remote_copy(
            src_ref=apart.at[c],
            dst_ref=a_in.at[c],
            send_sem=rs_s.at[c],
            recv_sem=rs_r.at[c],
            device_id=(u, to),
            device_id_type=MESH,
        )

    def ag_copy(b, to):
        return pltpu.make_async_remote_copy(
            src_ref=ou_ref.at[b],
            dst_ref=ou_ref.at[b],
            send_sem=ag_s.at[b],
            recv_sem=ag_r.at[b],
            device_id=(u, to),
            device_id_type=MESH,
        )

    def cc_copy(d):
        return pltpu.make_async_remote_copy(
            src_ref=cc_out,
            dst_ref=cc_in.at[d - 1],
            send_sem=cc_s.at[d - 1],
            recv_sem=cc_r.at[d - 1],
            device_id=(lax.rem(u + d, nu), z),
            device_id_type=MESH,
        )

    left = jnp.maximum(z - 1, 0)
    right = jnp.minimum(z + 1, ni - 1)

    for copy in inputs:
        copy.wait()

    for i in range(ib):
        rows = pl.ds(i * BLK, BLK)
        own = q_ref[rows, :]
        pair = both(own)
        qq[rows, :] = pair
        qg[i] = gram(stacked(own), pair)
    hs[...] = jnp.zeros_like(hs)
    for i in range(ib):
        present = p_ref[0, i]
        for b in range(1, ub):
            present = present + p_ref[b, i]
        cc_out[pl.ds(i, 1), :] = jnp.full((1, k), present.astype(f32), f32)

    pl.semaphore_wait(barrier, nu - 1 + jnp.minimum(z, 1) + jnp.minimum(ni - 1 - z, 1))

    def work_out(m):
        base = lax.rem(m + 1 - late, 2) * h
        for n in range(h):
            b = base + n
            total = p_ref[b, 0]
            grams = jnp.zeros((k, k), f32)
            for i in range(ib):
                present = p_ref[b, i].astype(f32)
                mask_row[n : n + 1, i * BLK : (i + 1) * BLK] = jnp.full((1, BLK), present, f32)
                grams = grams + present * qg[i]
                if i:
                    total = total + p_ref[b, i]
            packed, diagonal = pack(grams)
            gpart[b, 0:kh] = packed
            gpart[b, kh : kh + 1] = diagonal
            gpart[b, kh + 1 : kh + 8] = jnp.full((7, k), total.astype(f32), f32)

        @pl.when(jnp.logical_and(z == ni - 1, base == 0))
        def _():
            for n in range(h):
                g_copy(base + n, left).start()

        @pl.when(jnp.logical_and(z == 0, base == h))
        def _():
            for n in range(h):
                g_copy(base + n, right).start()

        for n in range(h):
            fetch(base + n).wait()
        for n in range(h):
            b = base + n
            rows = pl.ds(pl.multiple_of(b * BLK, BLK), BLK)
            masked[rows, :] = r_ref[b] * mask_row[n : n + 1, :].astype(bf16)
        rows = pl.ds(pl.multiple_of(base * BLK, BLK), h * BLK)
        a = fold(jnp.dot(masked[rows, :], qq[...], preferred_element_type=f32))
        for n in range(count):
            apart[PIECES * base + n] = a[n * piece : (n + 1) * piece]

        @pl.when(jnp.logical_and(z == ni - 1, base == 0))
        def _():
            for n in range(count):
                a_copy(PIECES * base + n, left).start()

        @pl.when(jnp.logical_and(z == 0, base == h))
        def _():
            for n in range(count):
                a_copy(PIECES * base + n, right).start()

    work_out(0)

    for d in range(1, nu):
        cc_copy(d).start()

    def prepare(b):
        g_three[b] = three(unpack(gpart[b, 0:kh], gpart[b, kh : kh + 1]))
        counted = 1.0 + gpart[b, kh + 1 : kh + 2]
        g_scale[b] = jnp.broadcast_to(step_ref[0] / (BLK * counted), (8, k))
        p = jnp.concatenate([u_ref[PIECES * b + n] for n in range(PIECES)], axis=0)
        known = times(p, g_three[b])
        for n in range(PIECES):
            foreseen[PIECES * b + n] = known[n * piece : (n + 1) * piece]

    def finish(c):
        b = c // PIECES
        s = g_scale[b, 0:1]
        d = apart[c] - foreseen[c]
        ou_ref[c] = u_ref[c] + s * (2.0 * d - s * times(d, g_three[b]))

    def use(b):
        own = jnp.concatenate([ou_ref[PIECES * b + n] for n in range(PIECES)], axis=0)
        stack = stacked(own)
        ppt[:, pl.ds(pl.multiple_of(b * BLK, BLK), BLK)] = stack
        g = gram(stack, both(own))
        for i in range(ib):
            hs[i] = hs[i] + p_ref[b, i].astype(f32) * g

    def valid(j, away, count):
        return jnp.logical_and(away, jnp.logical_and(j >= 0, j < count))

    def g_step(b, frm, to, last):
        g_copy(b, frm).wait_recv()
        gpart[b] = gpart[b] + g_in[b]

        @pl.when(jnp.logical_not(last))
        def _():
            g_copy(b, to).start()

        @pl.when(last)
        def _():
            prepare(b)

    def a_step(c, frm, to, last):
        a_copy(c, frm).wait_recv()
        apart[c] = apart[c] + a_in[c]

        @pl.when(jnp.logical_not(last))
        def _():
            a_copy(c, to).start()

        @pl.when(last)
        def _():
            finish(c)
            ag_copy(c, frm).start()

    def reduce_step(j, base, frm, to, away, last):
        @pl.when(valid(j, away, h + count))
        def _():
            @pl.when(j < h)
            def _():
                g_step(jnp.clip(j, 0, h - 1) + base * h, frm, to, last)

            @pl.when(j >= h)
            def _():
                a_step(low(j - h) + base * count, frm, to, last)

    def gather_step(j, c, frm, to, away, last):
        @pl.when(valid(j, away, count))
        def _():
            ag_copy(c, frm).wait_recv()

            @pl.when(jnp.logical_not(last))
            def _():
                ag_copy(c, to).start()

    def use_step(j, c, away):
        @pl.when(jnp.logical_and(valid(j, away, count), j % PIECES == PIECES - 1))
        def _():
            use(c // PIECES)

    far = LAG * (ni - 1)
    first, end = z == 0, z == ni - 1
    inner_first, inner_end = z > 0, z < ni - 1

    def low(j):
        return jnp.clip(j, 0, count - 1)

    def high(j):
        return low(j) + count

    turn = LAG * (ni // 2 - 1) + min(h, LAG) - 1
    if turn < LAG:
        work_out(1)

    @pl.loop(LAG, far + h + count)
    def _(t):
        reduce_step(t - LAG * z, 1, left, right, inner_first, end)
        reduce_step(t - (far - LAG * z), 0, right, left, inner_end, first)
        if turn >= LAG:

            @pl.when(t == turn)
            def _():
                work_out(1)

    @pl.when(jnp.logical_or(first, end))
    def _():
        @pl.loop(0, h)
        def _(n):
            use(n + jnp.minimum(z, 1) * h)

    for d in range(1, nu):
        cc_copy(d).wait_recv()
    counts = cc_out[...]
    for d in range(1, nu):
        counts = counts + cc_in[d - 1]
    scaling = step_ref[1] / (BLK * (1.0 + counts))
    for i in range(ib):
        scale[i * BLK : (i + 1) * BLK, :] = jnp.broadcast_to(scaling[i : i + 1], (BLK, k))

    @pl.loop(LAG, far + count)
    def _(t):
        gl = t - LAG * z
        gr = t - (far - LAG * z)
        gather_step(gl, low(gl), left, right, inner_first, end)
        gather_step(gr, high(gr), right, left, inner_end, first)
        use_step(gl, low(gl), inner_first)
        use_step(gr, high(gr), inner_end)

    bits = [(u // (1 << i)) % 2 for i in range(levels)]
    partners = [u + (1 << i) * (1 - 2 * bits[i]) for i in range(levels)]
    core = bits[0]

    def pick(xs, level, which):
        if level == 0:
            return xs[0]
        one, two = xs[level], xs[levels - level]
        return one + which * (two - one)

    mine = [pick(bits, n, core) for n in range(levels)]
    theirs = [pick(bits, n, 1 - core) for n in range(levels)]
    to = [pick(partners, n, core) for n in range(levels)]
    leaf = items >> levels
    offset = [sum(1 << (levels - m - 1) for m in range(n)) for n in range(levels)]

    def tails(level):
        return list(itertools.product((0, 1), repeat=levels - level - 1))

    def place(level, tail):
        number = 0
        for f in tail:
            number = 2 * number + f
        return offset[level] + number

    def rows_of(digits):
        start = 0
        for n, d in enumerate(digits):
            start = start + d * (items >> (n + 1))
        return pl.ds(pl.multiple_of(start, 8), leaf)

    def turned(known, tail):
        ahead = known[levels - len(tail) :] if tail else []
        return [1 - d if f else d for d, f in zip(ahead, tail)]

    def sent(level, tail):
        known = mine if level else theirs
        return rows_of(mine[:level] + [1 - mine[level]] + turned(known, tail))

    def held(level, tail):
        return rows_of(mine[: level + 1] + turned(mine, tail))

    def half_copy(level, tail):
        n = place(level, tail)
        return pltpu.make_async_remote_copy(
            src_ref=acc.at[sent(level, tail)],
            dst_ref=halves.at[n],
            send_sem=hv_s.at[n],
            recv_sem=hv_r.at[n],
            device_id=(to[level], z),
            device_id_type=MESH,
        )

    def double_copy(level, tail):
        n = place(level, tail)
        rows = held(level, tail)
        return pltpu.make_async_remote_copy(
            src_ref=oi_ref.at[rows],
            dst_ref=oi_ref.at[rows],
            send_sem=db_s.at[n],
            recv_sem=db_r.at[n],
            device_id=(to[level], z),
            device_id_type=MESH,
        )

    def product(base, n):
        base = pl.multiple_of(base, BLK)
        wide = jnp.dot(ppt[...], masked[:, pl.ds(base, n)], preferred_element_type=f32)
        wide = wide[:k] + wide[k:]
        for m in range(n // BLK):
            rows = pl.ds(pl.multiple_of(base + m * BLK, BLK), BLK)
            pair = qq[rows, :]
            left_side = jnp.concatenate([pair, pair[:, :k]], axis=1)
            known = jnp.dot(left_side, three(hs[base // BLK + m]), preferred_element_type=f32)
            acc[rows, :] = wide[:, m * BLK : (m + 1) * BLK].T - known

    quarter = items // 4
    for f in (1, 0):
        second = 1 - theirs[1] if f else theirs[1]
        product((1 - mine[0]) * 2 * quarter + second * quarter, quarter)
        for tail in reversed(tails(0)):
            if tail[0] == f:
                half_copy(0, tail).start()
    for level in range(levels):
        for tail in reversed(tails(level)):
            if level == 0 and all(tail[1:]):
                second = 1 - mine[1] if tail[0] else mine[1]
                product(mine[0] * 2 * quarter + second * quarter, quarter)
            half_copy(level, tail).wait_recv()
            rows = held(level, tail)
            summed = acc[rows, :] + halves[place(level, tail)]
            if tail:
                acc[rows, :] = summed
                if tail[0]:
                    half_copy(level + 1, tail[1:]).start()
            else:
                oi_ref[rows, :] = q_ref[rows, :] + summed * scale[rows, :]

    for level in reversed(range(levels)):
        double_copy(level, (0,) * (levels - level - 1)).start()
    for level in reversed(range(levels)):
        for tail in tails(level):
            double_copy(level, tail).wait_recv()
            for lower in reversed(range(level)):
                middle = (0,) * (level - lower - 1)
                double_copy(lower, middle + (1,) + tail).start()

    for level in range(levels):
        for tail in tails(level):
            half_copy(level, tail).wait_send()
            double_copy(level, tail).wait_send()
    for d in range(1, nu):
        cc_copy(d).wait_send()

    @pl.loop(0, count)
    def _(c):
        @pl.when(z > 0)
        def _():
            a_copy(c, left).wait_send()
            ag_copy(c + count, left).wait_send()

        @pl.when(z < ni - 1)
        def _():
            a_copy(c + count, right).wait_send()
            ag_copy(c, right).wait_send()

    @pl.loop(0, h)
    def _(b):
        @pl.when(z > 0)
        def _():
            g_copy(b, left).wait_send()

        @pl.when(z < ni - 1)
        def _():
            g_copy(b + h, right).wait_send()


def solution(mesh):
    nu, ni = mesh.shape["user"], mesh.shape["item"]

    def body(ratings, presence, user_factors, item_factors, step_sizes):
        users, items = ratings.shape
        k = item_factors.shape[1]
        ub, ib = users // BLK, items // BLK
        ibp = -(-ib // 8) * 8
        vm = pl.BlockSpec(memory_space=pltpu.VMEM)
        hbm = pl.BlockSpec(memory_space=pltpu.HBM)
        dma = pltpu.SemaphoreType.DMA
        new_users, new_items = pl.pallas_call(
            functools.partial(kernel, nu, ni),
            out_shape=(
                pltpu.VMEM((PIECES * ub, BLK // PIECES, k), f32),
                pltpu.VMEM((items, k), f32),
            ),
            in_specs=[hbm] * 5,
            out_specs=(vm, vm),
            scratch_shapes=[
                pltpu.VMEM((ub, BLK, items), bf16),
                pltpu.SMEM((ub, ib), jnp.int32),
                pltpu.VMEM((PIECES * ub, BLK // PIECES, k), f32),
                pltpu.VMEM((items, k), f32),
                pltpu.SMEM((2,), f32),
                pltpu.VMEM((items, 2 * k), bf16),
                pltpu.VMEM((ib, k, k), f32),
                pltpu.VMEM((users, items), bf16),
                pltpu.VMEM((-(-ub // 16) * 8, items), f32),
                pltpu.VMEM((ub, k // 2 + 8, k), f32),
                pltpu.VMEM((ub, k // 2 + 8, k), f32),
                pltpu.VMEM((PIECES * ub, BLK // PIECES, k), f32),
                pltpu.VMEM((PIECES * ub, BLK // PIECES, k), f32),
                pltpu.VMEM((ub, 3 * k, k), bf16),
                pltpu.VMEM((ub, 8, k), f32),
                pltpu.VMEM((PIECES * ub, BLK // PIECES, k), f32),
                pltpu.VMEM((2 * k, users), bf16),
                pltpu.VMEM((ib, k, k), f32),
                pltpu.VMEM((items, k), f32),
                pltpu.VMEM((items, k), f32),
                pltpu.VMEM((ibp, k), f32),
                pltpu.VMEM((nu - 1, ibp, k), f32),
                pltpu.VMEM((nu - 1, items // nu, k), f32),
                dma((4,)),
                dma((ub,)),
                dma((ub,)),
                dma((ub,)),
                dma((PIECES * ub,)),
                dma((PIECES * ub,)),
                dma((PIECES * ub,)),
                dma((PIECES * ub,)),
                dma((nu - 1,)),
                dma((nu - 1,)),
                dma((nu - 1,)),
                dma((nu - 1,)),
                dma((nu - 1,)),
                dma((nu - 1,)),
            ],
            compiler_params=pltpu.CompilerParams(
                collective_id=0, has_side_effects=True, vmem_limit_bytes=56 * 2**20
            ),
            cost_estimate=pl.CostEstimate(
                flops=8 * users * items * k, bytes_accessed=2 * users * items, transcendentals=0
            ),
        )(ratings, presence, user_factors.reshape(PIECES * ub, BLK // PIECES, k), item_factors, step_sizes)
        return new_users.reshape(users, k), new_items

    return jax.shard_map(
        body,
        mesh=mesh,
        in_specs=(P("user", "item"), P("user", "item"), P("user", None), P("item", None), P()),
        out_specs=(P("user", None), P("item", None)),
        check_vma=False,
    )
```

```python
import functools
import itertools

import jax
import jax.numpy as jnp
from jax import lax
from jax.experimental import pallas as pl
from jax.experimental.pallas import tpu as pltpu
from jax.sharding import PartitionSpec as P

BLK = 128
PIECES = 2
LAG = 7
f32 = jnp.float32
bf16 = jnp.bfloat16
MESH = pl.DeviceIdType.MESH


def split(x):
    hi = x.astype(bf16)
    lo = (x - hi.astype(f32)).astype(bf16)
    return hi, lo


def both(x):
    return jnp.concatenate(split(x), axis=1)


def fold(x):
    k = x.shape[1] // 2
    return x[:, :k] + x[:, k:]


def three(x):
    hi, lo = split(x)
    return jnp.concatenate([hi, hi, lo], axis=0)


def times(x, y_three):
    hi, lo = split(x)
    return jnp.dot(jnp.concatenate([hi, lo, hi], axis=1), y_three, preferred_element_type=f32)


def stacked(x):
    return jnp.concatenate(split(x.T), axis=0)


def gram(stack, pair):
    full = jnp.dot(stack, pair, preferred_element_type=f32)
    k = full.shape[0] // 2
    full = full[:k] + full[k:]
    return full[:, :k] + full[:, k:]


def grid_of(rows, k):
    row = lax.broadcasted_iota(jnp.int32, (rows, k), 0)
    lane = lax.broadcasted_iota(jnp.int32, (rows, k), 1)
    return row, lane


def pack(g):
    k = g.shape[0]
    n = k // 2
    row, lane = grid_of(n, k)
    low = g[n:]
    packed = jnp.where(lane < row, pltpu.roll(low, n, 1), g[:n])
    diagonal = jnp.sum(jnp.where(lane == row + n, low, 0.0), axis=0, keepdims=True)
    return packed, diagonal


def unpack(packed, diagonal):
    n, k = packed.shape
    row, lane = grid_of(n, k)
    upper = jnp.where(lane > row, packed, 0.0)
    lower = pltpu.roll(jnp.where(lane < row, packed, 0.0), n, 1)
    once = jnp.concatenate([upper, lower], axis=0)
    top = jnp.where(lane == row, packed, 0.0)
    bottom = jnp.where(lane == row + n, diagonal, 0.0)
    return once + once.T + jnp.concatenate([top, bottom], axis=0)


def kernel(
    nu,
    ni,
    r_hbm,
    p_hbm,
    u_hbm,
    q_hbm,
    step_hbm,
    ou_ref,
    oi_ref,
    r_ref,
    p_ref,
    u_ref,
    q_ref,
    step_ref,
    qq,
    qg,
    masked,
    mask_row,
    gpart,
    g_in,
    apart,
    a_in,
    g_three,
    g_scale,
    foreseen,
    ppt,
    hs,
    acc,
    scale,
    cc_out,
    cc_in,
    halves,
    *rest,
):
    levels = nu.bit_length() - 1
    (in_s, row_s, gs_s, gs_r, rs_s, rs_r, ag_s, ag_r, cc_s, cc_r, hv_s, hv_r, db_s, db_r) = rest
    ub, k = gpart.shape[0], gpart.shape[2]
    items = q_ref.shape[0]
    ib = items // BLK
    h = ub // 2
    piece = BLK // PIECES
    count = PIECES * h
    kh = k // 2
    u = lax.axis_index("user")
    z = lax.axis_index("item")

    inputs = [
        pltpu.make_async_copy(src, dst, in_s.at[n])
        for n, (src, dst) in enumerate(
            ((q_hbm, q_ref), (p_hbm, p_ref), (step_hbm, step_ref), (u_hbm, u_ref))
        )
    ]
    for copy in inputs:
        copy.start()

    def fetch(b):
        rows = pl.ds(pl.multiple_of(b * BLK, BLK), BLK)
        return pltpu.make_async_copy(r_hbm.at[rows], r_ref.at[b], row_s.at[b])

    late = z // ((ni + 1) // 2)

    def ordered(m):
        return lax.rem(m + (1 - late) * h, ub)

    for m in range(ub):
        fetch(ordered(m)).start()

    barrier = pltpu.get_barrier_semaphore()
    for d in range(1, nu):
        pl.semaphore_signal(barrier, inc=1, device_id=(lax.rem(u + d, nu), z), device_id_type=MESH)

    @pl.when(z > 0)
    def _():
        pl.semaphore_signal(barrier, inc=1, device_id=(u, z - 1), device_id_type=MESH)

    @pl.when(z < ni - 1)
    def _():
        pl.semaphore_signal(barrier, inc=1, device_id=(u, z + 1), device_id_type=MESH)

    def g_copy(b, to):
        return pltpu.make_async_remote_copy(
            src_ref=gpart.at[b],
            dst_ref=g_in.at[b],
            send_sem=gs_s.at[b],
            recv_sem=gs_r.at[b],
            device_id=(u, to),
            device_id_type=MESH,
        )

    def a_copy(c, to):
        return pltpu.make_async_remote_copy(
            src_ref=apart.at[c],
            dst_ref=a_in.at[c],
            send_sem=rs_s.at[c],
            recv_sem=rs_r.at[c],
            device_id=(u, to),
            device_id_type=MESH,
        )

    def ag_copy(b, to):
        return pltpu.make_async_remote_copy(
            src_ref=ou_ref.at[b],
            dst_ref=ou_ref.at[b],
            send_sem=ag_s.at[b],
            recv_sem=ag_r.at[b],
            device_id=(u, to),
            device_id_type=MESH,
        )

    def cc_copy(d):
        return pltpu.make_async_remote_copy(
            src_ref=cc_out,
            dst_ref=cc_in.at[d - 1],
            send_sem=cc_s.at[d - 1],
            recv_sem=cc_r.at[d - 1],
            device_id=(lax.rem(u + d, nu), z),
            device_id_type=MESH,
        )

    left = jnp.maximum(z - 1, 0)
    right = jnp.minimum(z + 1, ni - 1)

    for copy in inputs:
        copy.wait()

    for i in range(ib):
        rows = pl.ds(i * BLK, BLK)
        own = q_ref[rows, :]
        pair = both(own)
        qq[rows, :] = pair
        qg[i] = gram(stacked(own), pair)
    hs[...] = jnp.zeros_like(hs)
    for i in range(ib):
        present = p_ref[0, i]
        for b in range(1, ub):
            present = present + p_ref[b, i]
        cc_out[pl.ds(i, 1), :] = jnp.full((1, k), present.astype(f32), f32)

    pl.semaphore_wait(barrier, nu - 1 + jnp.minimum(z, 1) + jnp.minimum(ni - 1 - z, 1))

    def work_out(m):
        base = lax.rem(m + 1 - late, 2) * h
        for n in range(h):
            b = base + n
            total = p_ref[b, 0]
            grams = jnp.zeros((k, k), f32)
            for i in range(ib):
                present = p_ref[b, i].astype(f32)
                mask_row[n : n + 1, i * BLK : (i + 1) * BLK] = jnp.full((1, BLK), present, f32)
                grams = grams + present * qg[i]
                if i:
                    total = total + p_ref[b, i]
            packed, diagonal = pack(grams)
            gpart[b, 0:kh] = packed
            gpart[b, kh : kh + 1] = diagonal
            gpart[b, kh + 1 : kh + 8] = jnp.full((7, k), total.astype(f32), f32)

        @pl.when(jnp.logical_and(z == ni - 1, base == 0))
        def _():
            for n in range(h):
                g_copy(base + n, left).start()

        @pl.when(jnp.logical_and(z == 0, base == h))
        def _():
            for n in range(h):
                g_copy(base + n, right).start()

        for n in range(h):
            fetch(base + n).wait()
        for n in range(h):
            b = base + n
            rows = pl.ds(pl.multiple_of(b * BLK, BLK), BLK)
            masked[rows, :] = r_ref[b] * mask_row[n : n + 1, :].astype(bf16)
        rows = pl.ds(pl.multiple_of(base * BLK, BLK), h * BLK)
        a = fold(jnp.dot(masked[rows, :], qq[...], preferred_element_type=f32))
        for n in range(count):
            apart[PIECES * base + n] = a[n * piece : (n + 1) * piece]

        @pl.when(jnp.logical_and(z == ni - 1, base == 0))
        def _():
            for n in range(count):
                a_copy(PIECES * base + n, left).start()

        @pl.when(jnp.logical_and(z == 0, base == h))
        def _():
            for n in range(count):
                a_copy(PIECES * base + n, right).start()

    work_out(0)

    for d in range(1, nu):
        cc_copy(d).start()

    def prepare(b):
        g_three[b] = three(unpack(gpart[b, 0:kh], gpart[b, kh : kh + 1]))
        counted = 1.0 + gpart[b, kh + 1 : kh + 2]
        g_scale[b] = jnp.broadcast_to(step_ref[0] / (BLK * counted), (8, k))
        p = jnp.concatenate([u_ref[PIECES * b + n] for n in range(PIECES)], axis=0)
        known = times(p, g_three[b])
        for n in range(PIECES):
            foreseen[PIECES * b + n] = known[n * piece : (n + 1) * piece]

    def finish(c):
        b = c // PIECES
        s = g_scale[b, 0:1]
        d = apart[c] - foreseen[c]
        ou_ref[c] = u_ref[c] + s * (2.0 * d - s * times(d, g_three[b]))

    def use(b):
        own = jnp.concatenate([ou_ref[PIECES * b + n] for n in range(PIECES)], axis=0)
        stack = stacked(own)
        ppt[:, pl.ds(pl.multiple_of(b * BLK, BLK), BLK)] = stack
        g = gram(stack, both(own))
        for i in range(ib):
            hs[i] = hs[i] + p_ref[b, i].astype(f32) * g

    def valid(j, away, count):
        return jnp.logical_and(away, jnp.logical_and(j >= 0, j < count))

    def g_step(b, frm, to, last):
        g_copy(b, frm).wait_recv()
        gpart[b] = gpart[b] + g_in[b]

        @pl.when(jnp.logical_not(last))
        def _():
            g_copy(b, to).start()

        @pl.when(last)
        def _():
            prepare(b)

    def a_step(c, frm, to, last):
        a_copy(c, frm).wait_recv()
        apart[c] = apart[c] + a_in[c]

        @pl.when(jnp.logical_not(last))
        def _():
            a_copy(c, to).start()

        @pl.when(last)
        def _():
            finish(c)
            ag_copy(c, frm).start()

    def reduce_step(j, base, frm, to, away, last):
        @pl.when(valid(j, away, h + count))
        def _():
            @pl.when(j < h)
            def _():
                g_step(jnp.clip(j, 0, h - 1) + base * h, frm, to, last)

            @pl.when(j >= h)
            def _():
                a_step(low(j - h) + base * count, frm, to, last)

    def gather_step(j, c, frm, to, away, last):
        @pl.when(valid(j, away, count))
        def _():
            ag_copy(c, frm).wait_recv()

            @pl.when(jnp.logical_not(last))
            def _():
                ag_copy(c, to).start()

    def use_step(j, c, away):
        @pl.when(jnp.logical_and(valid(j, away, count), j % PIECES == PIECES - 1))
        def _():
            use(c // PIECES)

    far = LAG * (ni - 1)
    first, end = z == 0, z == ni - 1
    inner_first, inner_end = z > 0, z < ni - 1

    def low(j):
        return jnp.clip(j, 0, count - 1)

    def high(j):
        return low(j) + count

    turn = LAG * (ni // 2 - 1) + min(h, LAG) - 1
    if turn < LAG:
        work_out(1)

    @pl.loop(LAG, far + h + count)
    def _(t):
        reduce_step(t - LAG * z, 1, left, right, inner_first, end)
        reduce_step(t - (far - LAG * z), 0, right, left, inner_end, first)
        if turn >= LAG:

            @pl.when(t == turn)
            def _():
                work_out(1)

    @pl.when(jnp.logical_or(first, end))
    def _():
        @pl.loop(0, h)
        def _(n):
            use(n + jnp.minimum(z, 1) * h)

    for d in range(1, nu):
        cc_copy(d).wait_recv()
    counts = cc_out[...]
    for d in range(1, nu):
        counts = counts + cc_in[d - 1]
    scaling = step_ref[1] / (BLK * (1.0 + counts))
    for i in range(ib):
        scale[i * BLK : (i + 1) * BLK, :] = jnp.broadcast_to(scaling[i : i + 1], (BLK, k))

    @pl.loop(LAG, far + count)
    def _(t):
        gl = t - LAG * z
        gr = t - (far - LAG * z)
        gather_step(gl, low(gl), left, right, inner_first, end)
        gather_step(gr, high(gr), right, left, inner_end, first)
        use_step(gl, low(gl), inner_first)
        use_step(gr, high(gr), inner_end)

    bits = [(u // (1 << i)) % 2 for i in range(levels)]
    partners = [u + (1 << i) * (1 - 2 * bits[i]) for i in range(levels)]
    core = bits[0]

    def pick(xs, level, which):
        if level == 0:
            return xs[0]
        one, two = xs[level], xs[levels - level]
        return one + which * (two - one)

    mine = [pick(bits, n, core) for n in range(levels)]
    theirs = [pick(bits, n, 1 - core) for n in range(levels)]
    to = [pick(partners, n, core) for n in range(levels)]
    leaf = items >> levels
    offset = [sum(1 << (levels - m - 1) for m in range(n)) for n in range(levels)]

    def tails(level):
        return list(itertools.product((0, 1), repeat=levels - level - 1))

    def place(level, tail):
        number = 0
        for f in tail:
            number = 2 * number + f
        return offset[level] + number

    def rows_of(digits):
        start = 0
        for n, d in enumerate(digits):
            start = start + d * (items >> (n + 1))
        return pl.ds(pl.multiple_of(start, 8), leaf)

    def turned(known, tail):
        ahead = known[levels - len(tail) :] if tail else []
        return [1 - d if f else d for d, f in zip(ahead, tail)]

    def sent(level, tail):
        known = mine if level else theirs
        return rows_of(mine[:level] + [1 - mine[level]] + turned(known, tail))

    def held(level, tail):
        return rows_of(mine[: level + 1] + turned(mine, tail))

    def half_copy(level, tail):
        n = place(level, tail)
        return pltpu.make_async_remote_copy(
            src_ref=acc.at[sent(level, tail)],
            dst_ref=halves.at[n],
            send_sem=hv_s.at[n],
            recv_sem=hv_r.at[n],
            device_id=(to[level], z),
            device_id_type=MESH,
        )

    def double_copy(level, tail):
        n = place(level, tail)
        rows = held(level, tail)
        return pltpu.make_async_remote_copy(
            src_ref=oi_ref.at[rows],
            dst_ref=oi_ref.at[rows],
            send_sem=db_s.at[n],
            recv_sem=db_r.at[n],
            device_id=(to[level], z),
            device_id_type=MESH,
        )

    def product(base, n):
        base = pl.multiple_of(base, BLK)
        wide = jnp.dot(ppt[...], masked[:, pl.ds(base, n)], preferred_element_type=f32)
        wide = wide[:k] + wide[k:]
        for m in range(n // BLK):
            rows = pl.ds(pl.multiple_of(base + m * BLK, BLK), BLK)
            pair = qq[rows, :]
            left_side = jnp.concatenate([pair, pair[:, :k]], axis=1)
            known = jnp.dot(left_side, three(hs[base // BLK + m]), preferred_element_type=f32)
            acc[rows, :] = wide[:, m * BLK : (m + 1) * BLK].T - known

    quarter = items // 4
    for f in (1, 0):
        second = 1 - theirs[1] if f else theirs[1]
        product((1 - mine[0]) * 2 * quarter + second * quarter, quarter)
        for tail in reversed(tails(0)):
            if tail[0] == f:
                half_copy(0, tail).start()
    for level in range(levels):
        for tail in reversed(tails(level)):
            if level == 0 and all(tail[1:]):
                second = 1 - mine[1] if tail[0] else mine[1]
                product(mine[0] * 2 * quarter + second * quarter, quarter)
            half_copy(level, tail).wait_recv()
            rows = held(level, tail)
            summed = acc[rows, :] + halves[place(level, tail)]
            if tail:
                acc[rows, :] = summed
                if tail[0]:
                    half_copy(level + 1, tail[1:]).start()
            else:
                oi_ref[rows, :] = q_ref[rows, :] + summed * scale[rows, :]

    for level in reversed(range(levels)):
        double_copy(level, (0,) * (levels - level - 1)).start()
    for level in reversed(range(levels)):
        for tail in tails(level):
            double_copy(level, tail).wait_recv()
            for lower in reversed(range(level)):
                middle = (0,) * (level - lower - 1)
                double_copy(lower, middle + (1,) + tail).start()

    for level in range(levels):
        for tail in tails(level):
            half_copy(level, tail).wait_send()
            double_copy(level, tail).wait_send()
    for d in range(1, nu):
        cc_copy(d).wait_send()

    @pl.loop(0, count)
    def _(c):
        @pl.when(z > 0)
        def _():
            a_copy(c, left).wait_send()
            ag_copy(c + count, left).wait_send()

        @pl.when(z < ni - 1)
        def _():
            a_copy(c + count, right).wait_send()
            ag_copy(c, right).wait_send()

    @pl.loop(0, h)
    def _(b):
        @pl.when(z > 0)
        def _():
            g_copy(b, left).wait_send()

        @pl.when(z < ni - 1)
        def _():
            g_copy(b + h, right).wait_send()


def solution(mesh):
    nu, ni = mesh.shape["user"], mesh.shape["item"]

    def body(ratings, presence, user_factors, item_factors, step_sizes):
        users, items = ratings.shape
        k = item_factors.shape[1]
        ub, ib = users // BLK, items // BLK
        ibp = -(-ib // 8) * 8
        vm = pl.BlockSpec(memory_space=pltpu.VMEM)
        hbm = pl.BlockSpec(memory_space=pltpu.HBM)
        dma = pltpu.SemaphoreType.DMA
        new_users, new_items = pl.pallas_call(
            functools.partial(kernel, nu, ni),
            out_shape=(
                pltpu.VMEM((PIECES * ub, BLK // PIECES, k), f32),
                pltpu.VMEM((items, k), f32),
            ),
            in_specs=[hbm] * 5,
            out_specs=(vm, vm),
            scratch_shapes=[
                pltpu.VMEM((ub, BLK, items), bf16),
                pltpu.SMEM((ub, ib), jnp.int32),
                pltpu.VMEM((PIECES * ub, BLK // PIECES, k), f32),
                pltpu.VMEM((items, k), f32),
                pltpu.SMEM((2,), f32),
                pltpu.VMEM((items, 2 * k), bf16),
                pltpu.VMEM((ib, k, k), f32),
                pltpu.VMEM((users, items), bf16),
                pltpu.VMEM((-(-ub // 16) * 8, items), f32),
                pltpu.VMEM((ub, k // 2 + 8, k), f32),
                pltpu.VMEM((ub, k // 2 + 8, k), f32),
                pltpu.VMEM((PIECES * ub, BLK // PIECES, k), f32),
                pltpu.VMEM((PIECES * ub, BLK // PIECES, k), f32),
                pltpu.VMEM((ub, 3 * k, k), bf16),
                pltpu.VMEM((ub, 8, k), f32),
                pltpu.VMEM((PIECES * ub, BLK // PIECES, k), f32),
                pltpu.VMEM((2 * k, users), bf16),
                pltpu.VMEM((ib, k, k), f32),
                pltpu.VMEM((items, k), f32),
                pltpu.VMEM((items, k), f32),
                pltpu.VMEM((ibp, k), f32),
                pltpu.VMEM((nu - 1, ibp, k), f32),
                pltpu.VMEM((nu - 1, items // nu, k), f32),
                dma((4,)),
                dma((ub,)),
                dma((ub,)),
                dma((ub,)),
                dma((PIECES * ub,)),
                dma((PIECES * ub,)),
                dma((PIECES * ub,)),
                dma((PIECES * ub,)),
                dma((nu - 1,)),
                dma((nu - 1,)),
                dma((nu - 1,)),
                dma((nu - 1,)),
                dma((nu - 1,)),
                dma((nu - 1,)),
            ],
            compiler_params=pltpu.CompilerParams(
                collective_id=0, has_side_effects=True, vmem_limit_bytes=56 * 2**20
            ),
            cost_estimate=pl.CostEstimate(
                flops=8 * users * items * k, bytes_accessed=2 * users * items, transcendentals=0
            ),
        )(ratings, presence, user_factors.reshape(PIECES * ub, BLK // PIECES, k), item_factors, step_sizes)
        return new_users.reshape(users, k), new_items

    return jax.shard_map(
        body,
        mesh=mesh,
        in_specs=(P("user", "item"), P("user", "item"), P("user", None), P("item", None), P()),
        out_specs=(P("user", None), P("item", None)),
        check_vma=False,
    )
```
